128 devices in a mesh: sec: 4 (over x), site: 32 (over y, z, core).
Axes of the slice: x: 4, y: 4, z: 4, core: 2. Of those that a mesh axis runs over, the one named last changes fastest.
Arguments:
- tensors: bfloat16 [128, 4, 32, 4096], P(('sec', 'site')), may hold values from -6 to 6
- left_env: bfloat16 [128, 2, 32, 4096], P(('sec', 'site')), may hold values from -1.5 to 1.5, as said below
- right_env: bfloat16 [128, 2, 32, 4096], P(('sec', 'site')), may hold values from -1.5 to 1.5, as said below
- kept_rows: int32 [128, 32], P(('sec', 'site')), may hold values from 16 to 64
- coupling: float32 [4, 4], replicated, may hold values from -1 to 1
Outputs:
- new_tensors: bfloat16 [128, 4, 32, 4096], P(('sec', 'site'))
- new_left_env: bfloat16 [128, 2, 32, 4096], P(('sec', 'site'))
The draws below stay inside these ranges and needn't reach their ends.
Inputs may be any that keep to these rules, and one draw needn't show every extreme that they name: `left_env`: every 64 x 64 block is symmetric. `right_env`: every 64 x 64 block is symmetric.
All inputs are finite; a program needn't handle non-finite values.
Results may differ from the reference program's by a relative error of at most 0.01.
Values may be sent and summed in bfloat16 or wider, within the bound.
No kernel may reach another device: no remote copies, remote signals or barrier semaphores. Data moves between devices by JAX's collectives and lax.ppermute only.
A program may use at most 256 MiB of HBM per device.

```python
import jax
import jax.numpy as jnp
from jax import lax

NN = 8
NS = 4
BS = 64
PHYS = 4
ITERS = 4
NB = 32
CHAIN = 128


def symmetric_blocks(sample, spread):
    mirrored = (sample + jnp.swapaxes(sample, -1, -2)) * spread
    mirrored = jnp.clip(mirrored, -1.5, 1.5)
    return mirrored.reshape(CHAIN, 2, NB, BS * BS).astype(jnp.bfloat16)


def draw_left_env(key, part):
    key = jax.random.fold_in(key, 11)
    sample = jax.random.normal(key, (CHAIN, 2, NB, BS, BS), jnp.float32)
    return symmetric_blocks(sample, 0.18)


def draw_right_env(key, part):
    key = jax.random.fold_in(key, 23)
    sample = jax.random.normal(key, (CHAIN, 2, NB, BS, BS), jnp.float32)
    return symmetric_blocks(sample, 0.18)


def with_ends(result, rng, least, high):
    spot = [jax.random.randint(jax.random.fold_in(rng, axis), (), 0, length) for axis, length in enumerate(result.shape)]
    longest = result.shape.index(max(result.shape))
    neighbour = spot[:longest] + [(spot[longest] + 1) % result.shape[longest]] + spot[longest + 1:]
    return result.at[tuple(spot)].set(least).at[tuple(neighbour)].set(high)


def levels(key, extent, cuts, low, high):
    def one(dim, blocks):
        steps = jax.random.uniform(jax.random.fold_in(jax.random.fold_in(key, 6), dim), (blocks,), jnp.float32, low / len(cuts), high / len(cuts))
        return jnp.repeat(jnp.exp(steps), extent[dim] // blocks).reshape((-1,) + (1,) * (len(extent) - dim - 1))

    factor_of = one(*cuts[0])
    for cut in cuts[1:]:
        factor_of = factor_of * one(*cut)
    return factor_of


def centred(stream_key, shape, scale, reach, cuts=(), kind=jnp.bfloat16):
    array = jax.random.normal(stream_key, shape, jnp.float32) * scale
    if len(cuts) > 0:
        array = levels(stream_key, shape, cuts, -0.22, 0.18) * array
    return jnp.clip(array, min=-reach, max=reach).astype(kind)


def setup_inputs(seed: int = 0) -> dict:
    key_list = jax.random.split(jax.random.key(seed), 6)
    tensors = centred(key_list[0], (CHAIN, PHYS, NB, BS * BS), 1.0, 6.0, ((0, 128),))
    left_env = draw_left_env(jax.random.fold_in(key_list[5], 71), 0)
    right_env = draw_right_env(jax.random.fold_in(key_list[5], 71), 0)
    kept_rows = with_ends(jax.random.randint(key_list[3], (CHAIN, NB), BS // 4, BS + 1), jax.random.fold_in(key_list[3], 1), BS // 4, BS).astype(jnp.int32)
    coupling = jnp.clip(jax.random.uniform(key_list[4], (PHYS, PHYS), jnp.float32, -1.0, 1.0), -1.0, 1.0)
    return dict(tensors=tensors, left_env=left_env, right_env=right_env, kept_rows=kept_rows, coupling=coupling)


CHARGE_NUMBER = (0, 1, 1, 2)
CHARGE_SPIN = (0, 1, -1, 0)
OCCUPANCY = (0.0, 1.0, 1.0, 2.0)
STEP_SIZE = 0.06
EPSILON = 1e-06

def to_blocks(source):
    return source.reshape(source.shape[:-2] + (NN, NS, BS, BS))

def to_flat(source):
    return source.reshape(source.shape[:-4] + (NB, BS * BS))

def move_sectors(source, by_number, by_spin):
    return jnp.roll(source, (by_number, by_spin), axis=(-4, -3))

def rounded(source):
    return lax.optimization_barrier(source.astype(jnp.bfloat16)).astype(jnp.float32)

def pair_update(left_tensor, right_tensor, left_block, right_block, kept_row, coupling):
    tensor_left = to_blocks(left_tensor).astype(jnp.float32)
    tensor_right = to_blocks(right_tensor).astype(jnp.float32)
    env_left = to_blocks(left_block).astype(jnp.float32)
    env_right = to_blocks(right_block).astype(jnp.float32)
    pieces = []
    for left_state in range(PHYS):
        shifted = move_sectors(tensor_right, -CHARGE_NUMBER[left_state], -CHARGE_SPIN[left_state])
        pieces.append(jnp.einsum('nzab,tnzbc->tnzac', tensor_left[left_state], shifted))
    vector = rounded(jnp.stack(pieces))
    right_shifted = []
    for left_state in range(PHYS):
        column = []
        for right_state in range(PHYS):
            column.append(move_sectors(env_right, -(CHARGE_NUMBER[left_state] + CHARGE_NUMBER[right_state]), -(CHARGE_SPIN[left_state] + CHARGE_SPIN[right_state])))
        right_shifted.append(column)
    weights = coupling[:, :, None, None, None, None]
    for repeat in range(ITERS):
        applied = jnp.einsum('nzab,stnzbc->stnzac', env_left[0], vector) + weights * jnp.einsum('nzab,stnzbc->stnzac', env_left[1], vector)
        right_rows = []
        for left_state in range(PHYS):
            column = []
            for right_state in range(PHYS):
                moved = right_shifted[left_state][right_state]
                part = vector[left_state, right_state]
                column.append(jnp.einsum('nzab,nzbc->nzac', part, moved[0]) + coupling[left_state, right_state] * jnp.einsum('nzab,nzbc->nzac', part, moved[1]))
            right_rows.append(jnp.stack(column))
        applied = applied + jnp.stack(right_rows)
        quotient = jnp.sum(vector * applied) / jnp.sum(vector * vector)
        vector = rounded(vector - STEP_SIZE * (applied - quotient * vector))
    projected = jnp.zeros((PHYS, NN, NS, BS, BS), jnp.float32)
    for left_state in range(PHYS):
        contribution = jnp.einsum('nzba,tnzbc->tnzac', tensor_left[left_state], vector[left_state])
        projected = projected + move_sectors(contribution, CHARGE_NUMBER[left_state], CHARGE_SPIN[left_state])
    row_ids = jnp.arange(BS, dtype=jnp.int32)
    kept_mask = (row_ids[None, None, :] < kept_row.reshape(NN, NS)[:, :, None]).astype(jnp.float32)
    projected = projected * kept_mask[None, :, :, :, None]
    factor = lax.rsqrt(jnp.mean(projected * projected) + EPSILON)
    new_tensor = to_flat((projected * factor).astype(jnp.bfloat16))
    mixed_env = rounded(env_left[0] + env_left[1])
    total_energy = jnp.zeros((NN, NS, BS, BS), jnp.float32)
    total_density = jnp.zeros((NN, NS, BS, BS), jnp.float32)
    for left_state in range(PHYS):
        half_energy = rounded(jnp.einsum('nzba,nzbc->nzac', tensor_left[left_state], mixed_env))
        half_density = rounded(jnp.einsum('nzba,nzbc->nzac', tensor_left[left_state], env_left[1]))
        whole_energy = jnp.einsum('nzab,nzbc->nzac', half_energy, tensor_left[left_state])
        whole_density = jnp.einsum('nzab,nzbc->nzac', half_density, tensor_left[left_state])
        total_energy = total_energy + move_sectors(whole_energy, CHARGE_NUMBER[left_state], CHARGE_SPIN[left_state])
        total_density = total_density + OCCUPANCY[left_state] * move_sectors(whole_density, CHARGE_NUMBER[left_state], CHARGE_SPIN[left_state])
    new_env = to_flat((jnp.stack([total_energy, total_density]) / (PHYS * BS)).astype(jnp.bfloat16))
    return (new_tensor, new_env)

def reference(tensors, left_env, right_env, kept_rows, coupling):

    def update(pair_items):
        return pair_update(pair_items[0], pair_items[1], pair_items[2], pair_items[3], pair_items[4], coupling)
    made_tensors, made_envs = lax.map(update, (tensors[0::2], tensors[1::2], left_env[0::2], right_env[1::2], kept_rows[0::2]))
    tensors = tensors.at[1::2].set(made_tensors)
    left_env = left_env.at[1::2].set(made_envs)
    made_tensors, made_envs = lax.map(update, (tensors[1:-1:2], tensors[2::2], left_env[1:-1:2], right_env[2::2], kept_rows[1:-1:2]))
    tensors = tensors.at[2::2].set(made_tensors)
    left_env = left_env.at[2::2].set(made_envs)
    return (tensors, left_env)
```

```python
import functools

import jax
import jax.numpy as jnp
from jax import lax
from jax.experimental import pallas as pl
from jax.experimental.pallas import tpu as pltpu
from jax.sharding import PartitionSpec as P

NN = 8
NS = 4
BS = 64
PHYS = 4
ITERS = 4
NB = 32
CHARGE_NUMBER = (0, 1, 1, 2)
CHARGE_SPIN = (0, 1, -1, 0)
OCCUPANCY = (0.0, 1.0, 1.0, 2.0)
STEP_SIZE = 0.06
EPSILON = 1e-06
LN = PHYS * BS
UNROLL = 8
F32, BF16 = jnp.float32, jnp.bfloat16


def dot(a, b):
    return jnp.dot(a, b, preferred_element_type=F32)


def sector(q, number, spin):
    n = lax.rem(lax.div(q, NS) + number + NN, NN)
    z = lax.rem(lax.rem(q, NS) + spin + NS, NS)
    return n * NS + z


def plus(q, s):
    return sector(q, CHARGE_NUMBER[s], CHARGE_SPIN[s])


def minus(q, s):
    return sector(q, -CHARGE_NUMBER[s], -CHARGE_SPIN[s])


def bond_kernel(coup_ref, kept_ref, a_ref, b_ref, l_ref, r_ref, new_ref, env_ref, v, y, w, at):
    def weight_row(s1):
        lane = lax.broadcasted_iota(jnp.int32, (1, LN), 1)
        row = jnp.full((1, LN), coup_ref[s1, PHYS - 1], F32)
        for s2 in reversed(range(PHYS - 1)):
            row = jnp.where(lane < (s2 + 1) * BS, coup_ref[s1, s2], row)
        return row

    rows = [weight_row(s1) for s1 in range(PHYS)]
    rows16 = [row.astype(BF16) for row in rows]

    def build(q, _):
        zero = jnp.zeros((BS, BS), BF16)
        for ch in range(2):
            for s2 in range(PHYS):
                block = r_ref[ch, plus(q, s2)]
                parts = [block if t == s2 else zero for t in range(PHYS)]
                w[q, ch * LN + s2 * BS : ch * LN + (s2 + 1) * BS] = jnp.concatenate(parts, 1)
        for s1 in range(PHYS):
            at[q, :, s1 * BS : (s1 + 1) * BS] = a_ref[s1, minus(q, s1)].T
        cat = jnp.concatenate([b_ref[s2, q] for s2 in range(PHYS)], 1)
        for s1 in range(PHYS):
            p = minus(q, s1)
            v[s1, p] = dot(a_ref[s1, p], cat).astype(BF16)
        return 0

    lax.fori_loop(0, NB, build, 0, unroll=UNROLL)

    def fold(x):
        total = x[0:8]
        for i in range(1, BS // 8):
            total = total + x[i * 8 : (i + 1) * 8]
        return total

    quot = None
    for it in range(ITERS):

        def right(q, _, it=it, quot=quot):
            xs, cs = [], []
            for s1 in range(PHYS):
                p = minus(q, s1)
                if it:
                    old = v[s1, p].astype(F32)
                    x = (old - STEP_SIZE * (y[s1, p] - quot * old)).astype(BF16)
                    v[s1, p] = x
                else:
                    x = v[s1, p]
                xs.append(x)
                cs.append(x * rows16[s1])
            lhs = jnp.concatenate([jnp.concatenate(xs, 0), jnp.concatenate(cs, 0)], 1)
            out = dot(lhs, w[q])
            for s1 in range(PHYS):
                y[s1, minus(q, s1)] = out[s1 * BS : (s1 + 1) * BS]
            return 0

        lax.fori_loop(0, NB, right, 0, unroll=UNROLL)

        def left(q, carry):
            num, den = carry
            lhs = jnp.concatenate([l_ref[0, q], l_ref[1, q]], 1)
            for s1 in range(PHYS):
                x = v[s1, q]
                out = dot(lhs, jnp.concatenate([x, x * rows16[s1]], 0)) + y[s1, q]
                y[s1, q] = out
                wide = x.astype(F32)
                num = num + fold(wide * out)
                den = den + fold(wide * wide)
            return num, den

        zeros = jnp.zeros((8, LN), F32)
        num, den = lax.fori_loop(0, NB, left, (zeros, zeros), unroll=UNROLL)
        quot = jnp.sum(num, keepdims=True) / jnp.sum(den, keepdims=True)

    row_ids = lax.broadcasted_iota(jnp.int32, (BS, LN), 0)

    def project(p, total):
        parts = []
        for s1 in range(PHYS):
            q = minus(p, s1)
            old = v[s1, q].astype(F32)
            parts.append((old - STEP_SIZE * (y[s1, q] - quot * old)).astype(BF16))
        out = dot(at[p], jnp.concatenate(parts, 0))
        out = jnp.where(row_ids < kept_ref[0, p], out, 0.0)
        w2[p] = out
        return total + fold(out * out)

    w2 = y.at[0]

    def project_all(p, total):
        return project(p, total)

    total = lax.fori_loop(0, NB, project_all, jnp.zeros((8, LN), F32), unroll=UNROLL)
    factor = lax.rsqrt(jnp.sum(total, keepdims=True) / (PHYS * NB * BS * BS) + EPSILON)

    def finish(p, _):
        out = (w2[p] * factor).astype(BF16)
        for s2 in range(PHYS):
            new_ref[s2, p] = out[:, s2 * BS : (s2 + 1) * BS]
        e0, e1 = l_ref[0, p], l_ref[1, p]
        mixed = (e0.astype(F32) + e1.astype(F32)).astype(BF16)
        both = jnp.concatenate([mixed, e1], 1)
        for s1 in range(PHYS):
            t = plus(p, s1)
            half = dot(at[t, :, s1 * BS : (s1 + 1) * BS], both).astype(BF16)
            v[s1, t, :, : 2 * BS] = half
        return 0

    lax.fori_loop(0, NB, finish, 0, unroll=UNROLL)

    def grow(p, _):
        energy = jnp.concatenate([v[s, p, :, :BS] for s in range(PHYS)], 1)
        density = jnp.concatenate(
            [v[s, p, :, BS : 2 * BS] * BF16(OCCUPANCY[s]) for s in range(PHYS)], 1
        )
        stack = jnp.concatenate([a_ref[s, minus(p, s)] for s in range(PHYS)], 0)
        out = (dot(jnp.concatenate([energy, density], 0), stack) * (1.0 / (PHYS * BS))).astype(BF16)
        env_ref[0, p] = out[:BS]
        env_ref[1, p] = out[BS:]
        return 0

    lax.fori_loop(0, NB, grow, 0, unroll=UNROLL)


def bond(coupling, kept, a, b, left, right):
    vmem = pl.BlockSpec(memory_space=pltpu.VMEM)
    smem = pl.BlockSpec(memory_space=pltpu.SMEM)
    return pl.pallas_call(
        bond_kernel,
        out_shape=(
            jax.ShapeDtypeStruct((PHYS, NB, BS, BS), BF16),
            jax.ShapeDtypeStruct((2, NB, BS, BS), BF16),
        ),
        in_specs=[smem, smem, vmem, vmem, vmem, vmem],
        out_specs=(vmem, vmem),
        scratch_shapes=[
            pltpu.VMEM((PHYS, NB, BS, LN), BF16),
            pltpu.VMEM((PHYS, NB, BS, LN), F32),
            pltpu.VMEM((NB, 2 * LN, LN), BF16),
            pltpu.VMEM((NB, BS, LN), BF16),
        ],
        compiler_params=pltpu.CompilerParams(vmem_limit_bytes=60 * 2**20),
    )(coupling, kept, a, b, left, right)


def blocks(x):
    return x.reshape(x.shape[0], NB, BS, BS)


def flat(x):
    return x.reshape(x.shape[0], NB, BS * BS)


def shards(tensors, left_env, right_env, kept_rows, coupling):
    across = lax.axis_size("site")
    count = lax.axis_size("sec") * across
    position = lax.axis_index("sec") * across + lax.axis_index("site")
    axes = ("sec", "site")
    tensor, left, right = tensors[0], left_env[0], right_env[0]

    inward = [(i, i + 1) for i in range(0, count, 2)]
    back = [(i, i - 1) for i in range(2, count, 2)]
    ahead = [(i, i + 1) for i in range(1, count - 1, 2)]
    a1 = lax.ppermute(tensor, axes, inward)
    l1 = lax.ppermute(left, axes, inward)
    k1 = lax.ppermute(kept_rows, axes, inward)
    b2 = lax.ppermute(tensor, axes, back)
    r2 = lax.ppermute(right, axes, back)
    new1, env1 = bond(coupling, k1, blocks(a1), blocks(tensor), blocks(l1), blocks(right))
    new2, env2 = bond(coupling, kept_rows, new1, blocks(b2), env1, blocks(r2))
    got_new = lax.ppermute(flat(new2), axes, ahead)
    got_env = lax.ppermute(flat(env2), axes, ahead)
    odd = position % 2 == 1
    first = position == 0
    out_new = jnp.where(odd, flat(new1), jnp.where(first, tensor, got_new))
    out_env = jnp.where(odd, flat(env1), jnp.where(first, left, got_env))
    return out_new[None], out_env[None]


def solution(mesh):
    sites = P(("sec", "site"), None, None, None)
    return jax.shard_map(
        shards,
        mesh=mesh,
        in_specs=(sites, sites, sites, P(("sec", "site"), None), P()),
        out_specs=(sites, sites),
        check_vma=False,
    )
```

```python
import functools

import jax
import jax.numpy as jnp
from jax import lax
from jax.experimental import pallas as pl
from jax.experimental.pallas import tpu as pltpu
from jax.sharding import PartitionSpec as P

NN = 8
NS = 4
BS = 64
PHYS = 4
ITERS = 4
NB = 32
FLAT = BS * BS
CHARGE_NUMBER = (0, 1, 1, 2)
CHARGE_SPIN = (0, 1, -1, 0)
OCCUPANCY = (0.0, 1.0, 1.0, 2.0)
STEP_SIZE = 0.06
EPSILON = 1e-06
HALF = PHYS // 2
LN = HALF * BS
F32, BF16 = jnp.float32, jnp.bfloat16
LIMIT = 28 * 2**20
VM = pl.BlockSpec(memory_space=pltpu.VMEM)
SM = pl.BlockSpec(memory_space=pltpu.SMEM)
HB = pl.BlockSpec(memory_space=pl.ANY)


def dot(a, b):
    return jnp.dot(a, b, preferred_element_type=F32)


def sector(q, number, spin):
    return (q // NS + number) % NN * NS + (q % NS + spin) % NS


def plus(q, s):
    return sector(q, CHARGE_NUMBER[s], CHARGE_SPIN[s])


def minus(q, s):
    return sector(q, -CHARGE_NUMBER[s], -CHARGE_SPIN[s])


def fold(x):
    total = x[0:8]
    for i in range(1, BS // 8):
        total = total + x[i * 8 : (i + 1) * 8]
    return total


def scaled_copy(src, factor):
    return (src.astype(F32) * factor).astype(BF16)


def krylov_kernel(second, core_of, *refs):
    if second:
        coup, kept, own, got, b_even, b_odd, r_even, r_odd, left_raw = refs[:9]
        outs = refs[9:14]
        scratch = refs[14:]
    else:
        coup, kept, own, got, own_l, got_l, own_r, got_r = refs[:8]
        outs = refs[8:14]
        scratch = refs[14:]
    u, last, small, at, a_flat = outs[:5]
    a_raw, ab, lb, rb, bcat, w, sems, moments, b_raw, r_raw = scratch
    y = last
    core = core_of()

    if not second:
        left_raw = outs[5]

    def moves(odd):
        if second:
            mine = HALF if odd else 0
            pairs = [
                (own, a_raw.at[pl.ds(mine, HALF)]),
                (got, a_raw.at[pl.ds(HALF - mine, HALF)]),
                (b_odd if odd else b_even, b_raw),
                (r_odd if odd else r_even, r_raw),
            ]
        else:
            t_a, t_b = (got, own) if odd else (own, got)
            pairs = [
                (t_a, a_raw),
                (t_b.at[pl.ds(HALF if odd else 0, HALF)], b_raw),
                (got_l if odd else own_l, left_raw),
                (own_r if odd else got_r, r_raw),
            ]
        return [pltpu.make_async_copy(x, z, sems.at[i]) for i, (x, z) in enumerate(pairs)]

    for odd in (False, True):

        @pl.when(core == int(odd))
        def _(odd=odd):
            for copy in moves(odd):
                copy.start()
            for copy in moves(odd):
                copy.wait()

    lane = lax.broadcasted_iota(jnp.int32, (1, LN), 1)
    rows16 = [
        jnp.where(lane < BS, coup[s1, core * HALF], coup[s1, core * HALF + 1]).astype(BF16)
        for s1 in range(PHYS)
    ]

    for ch in range(2):
        rb[...] = r_raw[ch].reshape(NB, BS, BS)
        for q in range(NB):
            for h in range(HALF):
                low, high = plus(q, h), plus(q, HALF + h)
                block = rb[low + core * (high - low)]
                zero = jnp.zeros((BS, BS), BF16)
                parts = [block, zero] if h == 0 else [zero, block]
                w[q, ch * LN + h * BS : ch * LN + (h + 1) * BS] = jnp.concatenate(parts, 1)
    for ch in range(2):
        lb[:, :, ch * BS : (ch + 1) * BS] = left_raw[ch].reshape(NB, BS, BS)
    for h in range(HALF):
        bcat[:, :, h * BS : (h + 1) * BS] = b_raw[h].reshape(NB, BS, BS)

    if second:
        total = jnp.zeros((8, 128), F32)
        for s in range(PHYS):
            for t in range(FLAT // 128):
                x = a_raw[s, :, t * 128 : (t + 1) * 128].astype(F32)
                x = x * x
                total = total + (x[0:8] + x[8:16]) + (x[16:24] + x[24:32])
        factor = lax.rsqrt(jnp.sum(total, keepdims=True) / (PHYS * NB * FLAT) + EPSILON)
    for s in range(PHYS):
        x = a_raw[s]
        if second:
            x = scaled_copy(x, factor)
        a_flat[s] = x
        ab[s] = x.reshape(NB, BS, BS)

    for q in range(NB):
        for s1 in range(PHYS):
            at[q, :, s1 * BS : (s1 + 1) * BS] = ab[s1, minus(q, s1)].T
        lhs = jnp.concatenate([ab[s1, minus(q, s1)] for s1 in range(PHYS)], 0)
        out = dot(lhs, bcat[q]).astype(BF16)
        for s1 in range(PHYS):
            u[0, s1, minus(q, s1)] = out[s1 * BS : (s1 + 1) * BS]

    def product(it, _):
        now, later = u.at[it], u.at[it + 1]
        for q in range(NB):
            x = jnp.concatenate([now[s1, minus(q, s1)] for s1 in range(PHYS)], 0)
            c = jnp.concatenate([now[s1, minus(q, s1)] * rows16[s1] for s1 in range(PHYS)], 0)
            out = dot(jnp.concatenate([x, c], 1), w[q])
            for s1 in range(PHYS):
                y[s1, minus(q, s1)] = out[s1 * BS : (s1 + 1) * BS]
        even = jnp.zeros((8, LN), F32)
        odd = jnp.zeros((8, LN), F32)
        for q in range(NB):
            for pair in range(PHYS // 2):
                xs = [now[pair * 2 + j, q] for j in range(2)]
                cs = [xs[j] * rows16[pair * 2 + j] for j in range(2)]
                rhs = jnp.concatenate([jnp.concatenate(xs, 1), jnp.concatenate(cs, 1)], 0)
                out = dot(lb[q], rhs)
                for j in range(2):
                    s1 = pair * 2 + j
                    old = xs[j].astype(F32)
                    new = old - STEP_SIZE * (out[:, j * LN : (j + 1) * LN] + y[s1, q])
                    y[s1, q] = new
                    later[s1, q] = new.astype(BF16)
                    even = even + fold(old * old)
                    odd = odd + fold(old * new)
        moments[2 * it] = even
        moments[2 * it + 1] = odd
        return 0

    lax.fori_loop(0, ITERS, product, 0)

    row = lax.broadcasted_iota(jnp.int32, (8, 128), 0)
    column = lax.broadcasted_iota(jnp.int32, (8, 128), 1)
    out = jnp.zeros((8, 128), F32)
    for k in range(2 * ITERS):
        out = jnp.where((row == 0) & (column == k), jnp.sum(moments[k], keepdims=True), out)
    for q in range(NB):
        out = jnp.where((row == 1) & (column == q), kept[0, q].astype(F32), out)
    small[...] = out


def project_kernel(owner, core_of, own, got, u, last, at, x_out, v, xb):
    core = core_of()
    mine, other = own[...], got[...]
    both = mine + other
    row = lax.broadcasted_iota(jnp.int32, (8, 128), 0)
    column = lax.broadcasted_iota(jnp.int32, (8, 128), 1)

    def entry(array, r, c):
        return jnp.sum(jnp.where((row == r) & (column == c), array, 0.0), keepdims=True)

    t = [entry(both, 0, k) for k in range(2 * ITERS)]
    a = [jnp.ones((1, 1), F32)]
    for it in range(ITERS):
        den = sum(a[k] * a[j] * t[k + j] for k in range(it + 1) for j in range(it + 1))
        num = sum(a[k] * a[j] * t[k + j + 1] for k in range(it + 1) for j in range(it + 1))
        delta = 1.0 - num / den
        a = (
            [delta * a[0]]
            + [a[k - 1] + delta * a[k] for k in range(1, it + 1)]
            + [a[it]]
        )
    kept = jnp.where(core == owner, mine, other)
    row_ids = lax.broadcasted_iota(jnp.int32, (BS, LN), 0).astype(F32)
    for p in range(NB):
        parts = []
        for s1 in range(PHYS):
            q = minus(p, s1)
            total = last[s1, q]
            for k in range(ITERS):
                total = total + a[k] * u[k, s1, q].astype(F32)
            parts.append(total.astype(BF16))
        out = dot(at[p], jnp.concatenate(parts, 0))
        out = jnp.where(row_ids < entry(kept, 1, p), out, 0.0).astype(BF16)
        for h in range(HALF):
            xb[h, p] = out[:, h * BS : (h + 1) * BS]
    for h in range(HALF):
        x_out[h] = xb[h].reshape(NB, FLAT)


def env_kernel(a_flat, left, at, env, ab, lb, hb, eb):
    for s in range(PHYS):
        ab[s] = a_flat[s].reshape(NB, BS, BS)
    mixed = (left[0].astype(F32) + left[1].astype(F32)).astype(BF16)
    lb[:, :, :BS] = mixed.reshape(NB, BS, BS)
    lb[:, :, BS:] = left[1].reshape(NB, BS, BS)
    for q in range(NB):
        lhs = jnp.concatenate(
            [at[plus(q, s), :, s * BS : (s + 1) * BS] for s in range(PHYS)], 0
        )
        out = dot(lhs, lb[q]).astype(BF16)
        for s in range(PHYS):
            hb[s, q] = out[s * BS : (s + 1) * BS]
    for p in range(NB):
        halves = [hb[s, minus(p, s)] for s in range(PHYS)]
        energy = jnp.concatenate([half[:, :BS] for half in halves], 1)
        density = jnp.concatenate(
            [half[:, BS:] * BF16(OCCUPANCY[s]) for s, half in enumerate(halves)], 1
        )
        stack = jnp.concatenate([ab[s, minus(p, s)] for s in range(PHYS)], 0)
        out = dot(jnp.concatenate([energy, density], 0), stack) * (1.0 / (PHYS * BS))
        out = out.astype(BF16)
        eb[0, p] = out[:BS]
        eb[1, p] = out[BS:]
    for ch in range(2):
        env[ch] = eb[ch].reshape(NB, FLAT)


def shape(*dims, dtype=BF16):
    return jax.ShapeDtypeStruct(dims, dtype)


def params():
    return pltpu.CompilerParams(vmem_limit_bytes=LIMIT)


def krylov(core_of, second, coupling, kept, *arrays):
    outs = [
        shape(ITERS + 1, PHYS, NB, BS, LN),
        shape(PHYS, NB, BS, LN, dtype=F32),
        shape(8, 128, dtype=F32),
        shape(NB, BS, PHYS * BS),
        shape(PHYS, NB, FLAT),
    ]
    if not second:
        outs.append(shape(2, NB, FLAT))
    scratch = [
        pltpu.VMEM((PHYS, NB, FLAT), BF16),
        pltpu.VMEM((PHYS, NB, BS, BS), BF16),
        pltpu.VMEM((NB, BS, 2 * BS), BF16),
        pltpu.VMEM((NB, BS, BS), BF16),
        pltpu.VMEM((NB, BS, LN), BF16),
        pltpu.VMEM((NB, 2 * LN, LN), BF16),
        pltpu.SemaphoreType.DMA((4,)),
        pltpu.VMEM((2 * ITERS, 8, LN), F32),
        pltpu.VMEM((HALF, NB, FLAT), BF16),
        pltpu.VMEM((2, NB, FLAT), BF16),
    ]
    if second:
        specs = [SM, SM] + [HB] * 6 + [VM]
    else:
        specs = [SM, SM] + [HB] * 6
    return pl.pallas_call(
        functools.partial(krylov_kernel, second, core_of),
        out_shape=tuple(outs),
        in_specs=specs,
        out_specs=(VM,) * len(outs),
        scratch_shapes=scratch,
        compiler_params=params(),
        cost_estimate=pl.CostEstimate(flops=10**10, bytes_accessed=2**24, transcendentals=0),
        name="krylov",
    )(coupling, kept, *arrays)


def project(core_of, owner, own, got, u, last, at):
    return pl.pallas_call(
        functools.partial(project_kernel, owner, core_of),
        out_shape=shape(HALF, NB, FLAT),
        in_specs=[VM] * 5,
        out_specs=VM,
        scratch_shapes=[
            pltpu.VMEM((8, 128), F32),
            pltpu.VMEM((HALF, NB, BS, BS), BF16),
        ],
        compiler_params=params(),
        cost_estimate=pl.CostEstimate(flops=10**9, bytes_accessed=2**24, transcendentals=0),
        name="project",
    )(own, got, u, last, at)


def grow(a_flat, left, at):
    return pl.pallas_call(
        env_kernel,
        out_shape=shape(2, NB, FLAT),
        in_specs=[VM] * 3,
        out_specs=VM,
        scratch_shapes=[
            pltpu.VMEM((PHYS, NB, BS, BS), BF16),
            pltpu.VMEM((NB, BS, 2 * BS), BF16),
            pltpu.VMEM((PHYS, NB, BS, 2 * BS), BF16),
            pltpu.VMEM((2, NB, BS, BS), BF16),
        ],
        compiler_params=params(),
        cost_estimate=pl.CostEstimate(flops=10**9, bytes_accessed=2**22, transcendentals=0),
        name="grow",
    )(a_flat, left, at)


def core_index():
    return lax.rem(lax.axis_index("site"), 2)


def shards(tensors, left_env, right_env, kept_rows, coupling):
    across = lax.axis_size("site")
    count = lax.axis_size("sec") * across
    position = lax.axis_index("sec") * across + lax.axis_index("site")
    axes = ("sec", "site")
    tensor, left, right = tensors[0], left_env[0], right_env[0]

    swap = [(i, i ^ 1) for i in range(count)]
    rise = [(i, i + 1) for i in range(0, count, 2)]
    fall = [(i + 1, i) for i in range(0, count, 2)]
    to_even = [(i, i - 2) for i in range(2, count, 2)]
    to_odd = [(i, i - 1) for i in range(2, count, 2)]
    from_even = [(i, i + 2) for i in range(0, count - 2, 2)]
    from_odd = [(i, i + 1) for i in range(1, count - 2, 2)]

    def send(x, pairs):
        return lax.ppermute(x, axes, pairs)

    got_t = send(tensor, swap)
    got_l = send(left, rise)
    got_r = send(right, fall)
    late_t, late_r, got_t, got_l, got_r = lax.optimization_barrier(
        (tensor, right, got_t, got_l, got_r)
    )
    b_even = send(late_t[:HALF], to_even)
    r_even = send(late_r, to_even)
    b_odd = send(late_t[HALF:], to_odd)
    r_odd = send(late_r, to_odd)

    u, last, small, at, a_flat, l_flat = krylov(
        core_index, False, coupling, kept_rows, tensor, got_t, left, got_l, right, got_r
    )
    got_small = send(small, swap)
    env1 = grow(a_flat, l_flat, at)
    x = project(core_index, 0, small, got_small, u, last, at)
    got_x = send(x, swap)

    u, last, small, at, new1 = krylov(
        core_index, True, coupling, kept_rows, x, got_x, b_even, b_odd, r_even, r_odd, env1
    )
    got_small = send(small, swap)
    env2 = grow(new1, env1, at)
    x = project(core_index, 1, small, got_small, u, last, at)
    low = send(x, from_even)
    high = send(x, from_odd)
    got_env = send(env2, from_odd)

    squares = jnp.sum(jnp.square(low.astype(F32))) + jnp.sum(jnp.square(high.astype(F32)))
    factor = lax.rsqrt(squares / (PHYS * NB * FLAT) + EPSILON)
    received = scaled_copy(jnp.concatenate([low, high], 0), factor)
    odd = position % 2 == 1
    first = position == 0
    out_new = jnp.where(odd, new1, jnp.where(first, tensor, received))
    out_env = jnp.where(odd, env1, jnp.where(first, left, got_env))
    return out_new[None], out_env[None]


def solution(mesh):
    sites = P(("sec", "site"), None, None, None)
    return jax.shard_map(
        shards,
        mesh=mesh,
        in_specs=(sites, sites, sites, P(("sec", "site"), None), P()),
        out_specs=(sites, sites),
        check_vma=False,
    )
```

```python
import functools

import jax
import jax.numpy as jnp
from jax import lax
from jax.experimental import pallas as pl
from jax.experimental.pallas import tpu as pltpu
from jax.sharding import PartitionSpec as P

NN = 8
NS = 4
BS = 64
PHYS = 4
ITERS = 4
NB = 32
FLAT = BS * BS
CHARGE_NUMBER = (0, 1, 1, 2)
CHARGE_SPIN = (0, 1, -1, 0)
OCCUPANCY = (0.0, 1.0, 1.0, 2.0)
STEP_SIZE = 0.06
EPSILON = 1e-06
HALF = PHYS // 2
LN = HALF * BS
F32, BF16 = jnp.float32, jnp.bfloat16
MIB = 2**20
VM = pl.BlockSpec(memory_space=pltpu.VMEM)
SM = pl.BlockSpec(memory_space=pltpu.SMEM)
HB = pl.BlockSpec(memory_space=pltpu.HBM)


def dot(a, b):
    return jnp.dot(a, b, preferred_element_type=F32)


def sector(q, number, spin):
    return (q // NS + number) % NN * NS + (q % NS + spin) % NS


def plus(q, s):
    return sector(q, CHARGE_NUMBER[s], CHARGE_SPIN[s])


def minus(q, s):
    return sector(q, -CHARGE_NUMBER[s], -CHARGE_SPIN[s])


def fold(x):
    total = x[0:8]
    for i in range(1, BS // 8):
        total = total + x[i * 8 : (i + 1) * 8]
    return total


def scaled_copy(src, factor):
    return (src.astype(F32) * factor).astype(BF16)


def krylov_kernel(second, core_of, *refs):
    if second:
        coup, kept, own, got, b_even, b_odd, r_even, r_odd, left_raw = refs[:9]
        outs = refs[9:14]
        scratch = refs[14:]
    else:
        coup, kept, own, got, own_l, got_l, own_r, got_r = refs[:8]
        outs = refs[8:14]
        scratch = refs[14:]
    u, last, small, at, a_flat = outs[:5]
    a_raw, ab, lb, rb, bcat, w, sems, moments, b_raw, r_raw = scratch
    y = last
    core = core_of()

    if not second:
        left_raw = outs[5]

    def moves(odd):
        if second:
            mine = HALF if odd else 0
            pairs = [
                (own, a_raw.at[pl.ds(mine, HALF)]),
                (got, a_raw.at[pl.ds(HALF - mine, HALF)]),
                (b_odd if odd else b_even, b_raw),
                (r_odd if odd else r_even, r_raw),
            ]
        else:
            t_a, t_b = (got, own) if odd else (own, got)
            pairs = [
                (t_a, a_raw),
                (t_b.at[pl.ds(HALF if odd else 0, HALF)], b_raw),
                (got_l if odd else own_l, left_raw),
                (own_r if odd else got_r, r_raw),
            ]
        return [pltpu.make_async_copy(x, z, sems.at[i]) for i, (x, z) in enumerate(pairs)]

    for odd in (False, True):

        @pl.when(core == int(odd))
        def _(odd=odd):
            for copy in moves(odd):
                copy.start()
            for copy in moves(odd):
                copy.wait()

    lane = lax.broadcasted_iota(jnp.int32, (1, LN), 1)
    rows16 = [
        jnp.where(lane < BS, coup[s1, core * HALF], coup[s1, core * HALF + 1]).astype(BF16)
        for s1 in range(PHYS)
    ]

    for ch in range(2):
        rb[...] = r_raw[ch].reshape(NB, BS, BS)
        for q in range(NB):
            for h in range(HALF):
                low, high = plus(q, h), plus(q, HALF + h)
                block = rb[low + core * (high - low)]
                zero = jnp.zeros((BS, BS), BF16)
                parts = [block, zero] if h == 0 else [zero, block]
                w[q, ch * LN + h * BS : ch * LN + (h + 1) * BS] = jnp.concatenate(parts, 1)
    for ch in range(2):
        lb[:, :, ch * BS : (ch + 1) * BS] = left_raw[ch].reshape(NB, BS, BS)
    for h in range(HALF):
        bcat[:, :, h * BS : (h + 1) * BS] = b_raw[h].reshape(NB, BS, BS)

    if second:
        total = jnp.zeros((8, 128), F32)
        for s in range(PHYS):
            for t in range(FLAT // 128):
                x = a_raw[s, :, t * 128 : (t + 1) * 128].astype(F32)
                x = x * x
                total = total + (x[0:8] + x[8:16]) + (x[16:24] + x[24:32])
        factor = lax.rsqrt(jnp.sum(total, keepdims=True) / (PHYS * NB * FLAT) + EPSILON)
    for s in range(PHYS):
        x = a_raw[s]
        if second:
            x = scaled_copy(x, factor)
        a_flat[s] = x
        ab[s] = x.reshape(NB, BS, BS)

    for q in range(NB):
        for s1 in range(PHYS):
            at[q, :, s1 * BS : (s1 + 1) * BS] = ab[s1, minus(q, s1)].T
        lhs = jnp.concatenate([ab[s1, minus(q, s1)] for s1 in range(PHYS)], 0)
        out = dot(lhs, bcat[q]).astype(BF16)
        for s1 in range(PHYS):
            u[0, s1, minus(q, s1)] = out[s1 * BS : (s1 + 1) * BS]

    def product(it, _):
        now, later = u.at[it], u.at[it + 1]
        for q in range(NB):
            x = jnp.concatenate([now[s1, minus(q, s1)] for s1 in range(PHYS)], 0)
            c = jnp.concatenate([now[s1, minus(q, s1)] * rows16[s1] for s1 in range(PHYS)], 0)
            out = dot(jnp.concatenate([x, c], 1), w[q])
            for s1 in range(PHYS):
                y[s1, minus(q, s1)] = out[s1 * BS : (s1 + 1) * BS]
        even = jnp.zeros((8, LN), F32)
        odd = jnp.zeros((8, LN), F32)
        for q in range(NB):
            for pair in range(PHYS // 2):
                xs = [now[pair * 2 + j, q] for j in range(2)]
                cs = [xs[j] * rows16[pair * 2 + j] for j in range(2)]
                rhs = jnp.concatenate([jnp.concatenate(xs, 1), jnp.concatenate(cs, 1)], 0)
                out = dot(lb[q], rhs)
                for j in range(2):
                    s1 = pair * 2 + j
                    old = xs[j].astype(F32)
                    new = old - STEP_SIZE * (out[:, j * LN : (j + 1) * LN] + y[s1, q])
                    y[s1, q] = new
                    later[s1, q] = new.astype(BF16)
                    even = even + fold(old * old)
                    odd = odd + fold(old * new)
        moments[2 * it] = even
        moments[2 * it + 1] = odd
        return 0

    lax.fori_loop(0, ITERS, product, 0)

    row = lax.broadcasted_iota(jnp.int32, (8, 128), 0)
    column = lax.broadcasted_iota(jnp.int32, (8, 128), 1)
    out = jnp.zeros((8, 128), F32)
    for k in range(2 * ITERS):
        out = jnp.where((row == 0) & (column == k), jnp.sum(moments[k], keepdims=True), out)
    for q in range(NB):
        out = jnp.where((row == 1) & (column == q), kept[0, q].astype(F32), out)
    small[...] = out


def project_kernel(owner, core_of, own, got, u, last, at, x_out, v, xb):
    core = core_of()
    mine, other = own[...], got[...]
    both = mine + other
    row = lax.broadcasted_iota(jnp.int32, (8, 128), 0)
    column = lax.broadcasted_iota(jnp.int32, (8, 128), 1)

    def entry(array, r, c):
        return jnp.sum(jnp.where((row == r) & (column == c), array, 0.0), keepdims=True)

    t = [entry(both, 0, k) for k in range(2 * ITERS)]
    a = [jnp.ones((1, 1), F32)]
    for it in range(ITERS):
        den = sum(a[k] * a[j] * t[k + j] for k in range(it + 1) for j in range(it + 1))
        num = sum(a[k] * a[j] * t[k + j + 1] for k in range(it + 1) for j in range(it + 1))
        delta = 1.0 - num / den
        a = (
            [delta * a[0]]
            + [a[k - 1] + delta * a[k] for k in range(1, it + 1)]
            + [a[it]]
        )
    kept = jnp.where(core == owner, mine, other)
    row_ids = lax.broadcasted_iota(jnp.int32, (BS, LN), 0).astype(F32)
    for p in range(NB):
        parts = []
        for s1 in range(PHYS):
            q = minus(p, s1)
            total = last[s1, q]
            for k in range(ITERS):
                total = total + a[k] * u[k, s1, q].astype(F32)
            parts.append(total.astype(BF16))
        out = dot(at[p], jnp.concatenate(parts, 0))
        out = jnp.where(row_ids < entry(kept, 1, p), out, 0.0).astype(BF16)
        for h in range(HALF):
            xb[h, p] = out[:, h * BS : (h + 1) * BS]
    for h in range(HALF):
        x_out[h] = xb[h].reshape(NB, FLAT)


def env_kernel(a_flat, left, at, env, ab, lb, hb, eb):
    for s in range(PHYS):
        ab[s] = a_flat[s].reshape(NB, BS, BS)
    mixed = (left[0].astype(F32) + left[1].astype(F32)).astype(BF16)
    lb[:, :, :BS] = mixed.reshape(NB, BS, BS)
    lb[:, :, BS:] = left[1].reshape(NB, BS, BS)
    for q in range(NB):
        lhs = jnp.concatenate(
            [at[plus(q, s), :, s * BS : (s + 1) * BS] for s in range(PHYS)], 0
        )
        out = dot(lhs, lb[q]).astype(BF16)
        for s in range(PHYS):
            hb[s, q] = out[s * BS : (s + 1) * BS]
    for p in range(NB):
        halves = [hb[s, minus(p, s)] for s in range(PHYS)]
        energy = jnp.concatenate([half[:, :BS] for half in halves], 1)
        density = jnp.concatenate(
            [half[:, BS:] * BF16(OCCUPANCY[s]) for s, half in enumerate(halves)], 1
        )
        stack = jnp.concatenate([ab[s, minus(p, s)] for s in range(PHYS)], 0)
        out = dot(jnp.concatenate([energy, density], 0), stack) * (1.0 / (PHYS * BS))
        out = out.astype(BF16)
        eb[0, p] = out[:BS]
        eb[1, p] = out[BS:]
    for ch in range(2):
        env[ch] = eb[ch].reshape(NB, FLAT)


def shape(*dims, dtype=BF16):
    return jax.ShapeDtypeStruct(dims, dtype)


def params(size):
    return pltpu.CompilerParams(vmem_limit_bytes=size * MIB)


def krylov(core_of, second, coupling, kept, *arrays):
    outs = [
        shape(ITERS + 1, PHYS, NB, BS, LN),
        shape(PHYS, NB, BS, LN, dtype=F32),
        shape(8, 128, dtype=F32),
        shape(NB, BS, PHYS * BS),
        shape(PHYS, NB, FLAT),
    ]
    if not second:
        outs.append(shape(2, NB, FLAT))
    scratch = [
        pltpu.VMEM((PHYS, NB, FLAT), BF16),
        pltpu.VMEM((PHYS, NB, BS, BS), BF16),
        pltpu.VMEM((NB, BS, 2 * BS), BF16),
        pltpu.VMEM((NB, BS, BS), BF16),
        pltpu.VMEM((NB, BS, LN), BF16),
        pltpu.VMEM((NB, 2 * LN, LN), BF16),
        pltpu.SemaphoreType.DMA((4,)),
        pltpu.VMEM((2 * ITERS, 8, LN), F32),
        pltpu.VMEM((HALF, NB, FLAT), BF16),
        pltpu.VMEM((2, NB, FLAT), BF16),
    ]
    if second:
        specs = [SM, SM] + [HB] * 6 + [VM]
    else:
        specs = [SM, SM] + [HB] * 6
    return pl.pallas_call(
        functools.partial(krylov_kernel, second, core_of),
        out_shape=tuple(outs),
        in_specs=specs,
        out_specs=(VM,) * len(outs),
        scratch_shapes=scratch,
        compiler_params=params(28),
        cost_estimate=pl.CostEstimate(flops=10**11, bytes_accessed=2**24, transcendentals=0),
        name="krylov",
    )(coupling, kept, *arrays)


def project(core_of, owner, own, got, u, last, at):
    return pl.pallas_call(
        functools.partial(project_kernel, owner, core_of),
        out_shape=shape(HALF, NB, FLAT),
        in_specs=[VM] * 5,
        out_specs=VM,
        scratch_shapes=[
            pltpu.VMEM((8, 128), F32),
            pltpu.VMEM((HALF, NB, BS, BS), BF16),
        ],
        compiler_params=params(20),
        cost_estimate=pl.CostEstimate(flops=10**6, bytes_accessed=2**10, transcendentals=0),
        name="project",
    )(own, got, u, last, at)


def grow(a_flat, left, at):
    return pl.pallas_call(
        env_kernel,
        out_shape=shape(2, NB, FLAT),
        in_specs=[VM] * 3,
        out_specs=VM,
        scratch_shapes=[
            pltpu.VMEM((PHYS, NB, BS, BS), BF16),
            pltpu.VMEM((NB, BS, 2 * BS), BF16),
            pltpu.VMEM((PHYS, NB, BS, 2 * BS), BF16),
            pltpu.VMEM((2, NB, BS, BS), BF16),
        ],
        compiler_params=params(12),
        cost_estimate=pl.CostEstimate(flops=10**6, bytes_accessed=2**10, transcendentals=0),
        name="grow",
    )(a_flat, left, at)


def core_index():
    return lax.rem(lax.axis_index("site"), 2)


def shards(tensors, left_env, right_env, kept_rows, coupling):
    across = lax.axis_size("site")
    count = lax.axis_size("sec") * across
    position = lax.axis_index("sec") * across + lax.axis_index("site")
    axes = ("sec", "site")
    tensor, left, right = tensors[0], left_env[0], right_env[0]

    swap = [(i, i ^ 1) for i in range(count)]
    rise = [(i, i + 1) for i in range(0, count, 2)]
    fall = [(i + 1, i) for i in range(0, count, 2)]
    to_even = [(i, i - 2) for i in range(2, count, 2)]
    to_odd = [(i, i - 1) for i in range(2, count, 2)]
    from_even = [(i, i + 2) for i in range(0, count - 2, 2)]
    from_odd = [(i, i + 1) for i in range(1, count - 2, 2)]

    def send(x, pairs):
        return lax.ppermute(x, axes, pairs)

    got_t = send(tensor, swap)
    got_l = send(left, rise)
    got_r = send(right, fall)
    low, high, late_r, got_t, got_l, got_r = lax.optimization_barrier(
        (tensor[:HALF], tensor[HALF:], right, got_t, got_l, got_r)
    )
    b_even = send(low, to_even)
    b_odd = send(high, to_odd)
    r_even = send(late_r, to_even)
    r_odd = send(late_r, to_odd)

    u, last, small, at, a_flat, l_flat = krylov(
        core_index, False, coupling, kept_rows, tensor, got_t, left, got_l, right, got_r
    )
    got_small = send(small, swap)
    env1 = grow(a_flat, l_flat, at)
    x = project(core_index, 0, small, got_small, u, last, at)
    x, b_even, b_odd, r_even, r_odd = lax.optimization_barrier((x, b_even, b_odd, r_even, r_odd))
    got_x = send(x, swap)

    u, last, small, at, new1 = krylov(
        core_index, True, coupling, kept_rows, x, got_x, b_even, b_odd, r_even, r_odd, env1
    )
    got_small = send(small, swap)
    env2 = grow(new1, env1, at)
    x = project(core_index, 1, small, got_small, u, last, at)
    low = send(x, from_even)
    high = send(x, from_odd)
    got_env = send(env2, from_odd)

    squares = jnp.sum(jnp.square(low.astype(F32))) + jnp.sum(jnp.square(high.astype(F32)))
    factor = lax.rsqrt(squares / (PHYS * NB * FLAT) + EPSILON)
    received = scaled_copy(jnp.concatenate([low, high], 0), factor)
    odd = position % 2 == 1
    first = position == 0
    out_new = jnp.where(odd, new1, jnp.where(first, tensor, received))
    out_env = jnp.where(odd, env1, jnp.where(first, left, got_env))
    return out_new[None], out_env[None]


def solution(mesh):
    sites = P(("sec", "site"), None, None, None)
    return jax.shard_map(
        shards,
        mesh=mesh,
        in_specs=(sites, sites, sites, P(("sec", "site"), None), P()),
        out_specs=(sites, sites),
        check_vma=False,
    )
```

```python
import functools

import jax
import jax.numpy as jnp
from jax import lax
from jax.experimental import pallas as pl
from jax.experimental.pallas import tpu as pltpu
from jax.sharding import PartitionSpec as P

NN = 8
NS = 4
BS = 64
PHYS = 4
ITERS = 4
NB = 32
FLAT = BS * BS
CHARGE_NUMBER = (0, 1, 1, 2)
CHARGE_SPIN = (0, 1, -1, 0)
OCCUPANCY = (0.0, 1.0, 1.0, 2.0)
STEP_SIZE = 0.06
EPSILON = 1e-06
HALF = PHYS // 2
LN = HALF * BS
F32, BF16 = jnp.float32, jnp.bfloat16
MIB = 2**20
VM = pl.BlockSpec(memory_space=pltpu.VMEM)
SM = pl.BlockSpec(memory_space=pltpu.SMEM)
HB = pl.BlockSpec(memory_space=pltpu.HBM)


def dot(a, b):
    return jnp.dot(a, b, preferred_element_type=F32)


def sector(q, number, spin):
    return (q // NS + number) % NN * NS + (q % NS + spin) % NS


def plus(q, s):
    return sector(q, CHARGE_NUMBER[s], CHARGE_SPIN[s])


def minus(q, s):
    return sector(q, -CHARGE_NUMBER[s], -CHARGE_SPIN[s])


def fold(x):
    total = x[0:8]
    for i in range(1, BS // 8):
        total = total + x[i * 8 : (i + 1) * 8]
    return total


def scaled_copy(src, factor):
    return (src.astype(F32) * factor).astype(BF16)


def krylov_kernel(second, core_of, *refs):
    if second:
        coup, kept, own, got, b_even, b_odd, r_even, r_odd, left_raw = refs[:9]
        outs = refs[9:15]
        scratch = refs[15:]
    else:
        coup, kept, own, got, own_l, got_l, own_r, got_r = refs[:8]
        outs = refs[8:14]
        scratch = refs[14:]
    u, last, small, at, a_flat = outs[:5]
    a_raw, ab, lb, rb, bcat, w, sems, moments, b_raw, r_raw, eb = scratch
    y = last
    core = core_of()

    if not second:
        left_raw = outs[5]

    def moves(odd):
        if second:
            mine = HALF if odd else 0
            pairs = [
                (own, a_raw.at[pl.ds(mine, HALF)]),
                (got, a_raw.at[pl.ds(HALF - mine, HALF)]),
                (b_odd if odd else b_even, b_raw),
                (r_odd if odd else r_even, r_raw),
            ]
        else:
            t_a, t_b = (got, own) if odd else (own, got)
            pairs = [
                (t_a, a_raw),
                (t_b.at[pl.ds(HALF if odd else 0, HALF)], b_raw),
                (got_l if odd else own_l, left_raw),
                (own_r if odd else got_r, r_raw),
            ]
        return [pltpu.make_async_copy(x, z, sems.at[i]) for i, (x, z) in enumerate(pairs)]

    for odd in (False, True):

        @pl.when(core == int(odd))
        def _(odd=odd):
            for copy in moves(odd):
                copy.start()
            for copy in moves(odd):
                copy.wait()

    lane = lax.broadcasted_iota(jnp.int32, (1, LN), 1)
    rows16 = [
        jnp.where(lane < BS, coup[s1, core * HALF], coup[s1, core * HALF + 1]).astype(BF16)
        for s1 in range(PHYS)
    ]

    for ch in range(2):
        rb[...] = r_raw[ch].reshape(NB, BS, BS)
        for q in range(NB):
            for h in range(HALF):
                low, high = plus(q, h), plus(q, HALF + h)
                block = rb[low + core * (high - low)]
                zero = jnp.zeros((BS, BS), BF16)
                parts = [block, zero] if h == 0 else [zero, block]
                w[q, ch * LN + h * BS : ch * LN + (h + 1) * BS] = jnp.concatenate(parts, 1)
    for ch in range(2):
        lb[:, :, ch * BS : (ch + 1) * BS] = left_raw[ch].reshape(NB, BS, BS)
    for h in range(HALF):
        bcat[:, :, h * BS : (h + 1) * BS] = b_raw[h].reshape(NB, BS, BS)

    if second:
        factor = norm_factor(sum_squares(a_raw, PHYS))
    for s in range(PHYS):
        x = a_raw[s]
        if second:
            x = scaled_copy(x, factor)
        a_flat[s] = x
        ab[s] = x.reshape(NB, BS, BS)

    for q in range(NB):
        for s1 in range(PHYS):
            at[q, :, s1 * BS : (s1 + 1) * BS] = ab[s1, minus(q, s1)].T
        lhs = jnp.concatenate([ab[s1, minus(q, s1)] for s1 in range(PHYS)], 0)
        out = dot(lhs, bcat[q]).astype(BF16)
        for s1 in range(PHYS):
            u[0, s1, minus(q, s1)] = out[s1 * BS : (s1 + 1) * BS]

    def product(it, _):
        now, later = u.at[it], u.at[it + 1]
        for q in range(NB):
            x = jnp.concatenate([now[s1, minus(q, s1)] for s1 in range(PHYS)], 0)
            c = jnp.concatenate([now[s1, minus(q, s1)] * rows16[s1] for s1 in range(PHYS)], 0)
            out = dot(jnp.concatenate([x, c], 1), w[q])
            for s1 in range(PHYS):
                y[s1, minus(q, s1)] = out[s1 * BS : (s1 + 1) * BS]
        even = jnp.zeros((8, LN), F32)
        odd = jnp.zeros((8, LN), F32)
        for q in range(NB):
            for pair in range(PHYS // 2):
                xs = [now[pair * 2 + j, q] for j in range(2)]
                cs = [xs[j] * rows16[pair * 2 + j] for j in range(2)]
                rhs = jnp.concatenate([jnp.concatenate(xs, 1), jnp.concatenate(cs, 1)], 0)
                out = dot(lb[q], rhs)
                for j in range(2):
                    s1 = pair * 2 + j
                    old = xs[j].astype(F32)
                    new = old - STEP_SIZE * (out[:, j * LN : (j + 1) * LN] + y[s1, q])
                    y[s1, q] = new
                    later[s1, q] = new.astype(BF16)
                    even = even + fold(old * old)
                    odd = odd + fold(old * new)
        moments[2 * it] = even
        moments[2 * it + 1] = odd
        return 0

    lax.fori_loop(0, ITERS, product, 0)

    row = lax.broadcasted_iota(jnp.int32, (8, 128), 0)
    column = lax.broadcasted_iota(jnp.int32, (8, 128), 1)
    out = jnp.zeros((8, 128), F32)
    for k in range(2 * ITERS):
        out = jnp.where((row == 0) & (column == k), jnp.sum(moments[k], keepdims=True), out)
    for q in range(NB):
        out = jnp.where((row == 1) & (column == q), kept[0, q].astype(F32), out)
    small[...] = out
    if second:
        env_part(left_raw, at, outs[5], ab, lb, u.at[ITERS], eb)


def project_kernel(owner, core_of, own, got, u, last, at, x_out, v, xb):
    core = core_of()
    mine, other = own[...], got[...]
    both = mine + other
    row = lax.broadcasted_iota(jnp.int32, (8, 128), 0)
    column = lax.broadcasted_iota(jnp.int32, (8, 128), 1)

    def entry(array, r, c):
        return jnp.sum(jnp.where((row == r) & (column == c), array, 0.0), keepdims=True)

    t = [entry(both, 0, k) for k in range(2 * ITERS)]
    a = [jnp.ones((1, 1), F32)]
    for it in range(ITERS):
        den = sum(a[k] * a[j] * t[k + j] for k in range(it + 1) for j in range(it + 1))
        num = sum(a[k] * a[j] * t[k + j + 1] for k in range(it + 1) for j in range(it + 1))
        delta = 1.0 - num / den
        a = (
            [delta * a[0]]
            + [a[k - 1] + delta * a[k] for k in range(1, it + 1)]
            + [a[it]]
        )
    kept = jnp.where(core == owner, mine, other)
    row_ids = lax.broadcasted_iota(jnp.int32, (BS, LN), 0).astype(F32)
    for p in range(NB):
        parts = []
        for s1 in range(PHYS):
            q = minus(p, s1)
            total = last[s1, q]
            for k in range(ITERS):
                total = total + a[k] * u[k, s1, q].astype(F32)
            parts.append(total.astype(BF16))
        out = dot(at[p], jnp.concatenate(parts, 0))
        out = jnp.where(row_ids < entry(kept, 1, p), out, 0.0).astype(BF16)
        for h in range(HALF):
            xb[h, p] = out[:, h * BS : (h + 1) * BS]
    for h in range(HALF):
        x_out[h] = xb[h].reshape(NB, FLAT)


def env_part(left, at, env, ab, lb, hb, eb):
    mixed = (left[0].astype(F32) + left[1].astype(F32)).astype(BF16)
    lb[:, :, :BS] = mixed.reshape(NB, BS, BS)
    for q in range(NB):
        lhs = jnp.concatenate(
            [at[plus(q, s), :, s * BS : (s + 1) * BS] for s in range(PHYS)], 0
        )
        out = dot(lhs, lb[q]).astype(BF16)
        for s in range(PHYS):
            hb[s, q] = out[s * BS : (s + 1) * BS]
    for p in range(NB):
        halves = [hb[s, minus(p, s)] for s in range(PHYS)]
        energy = jnp.concatenate([half[:, :BS] for half in halves], 1)
        density = jnp.concatenate(
            [half[:, BS:] * BF16(OCCUPANCY[s]) for s, half in enumerate(halves)], 1
        )
        stack = jnp.concatenate([ab[s, minus(p, s)] for s in range(PHYS)], 0)
        out = dot(jnp.concatenate([energy, density], 0), stack) * (1.0 / (PHYS * BS))
        out = out.astype(BF16)
        eb[0, p] = out[:BS]
        eb[1, p] = out[BS:]
    for ch in range(2):
        env[ch] = eb[ch].reshape(NB, FLAT)


def env_kernel(a_flat, left, at, env, ab, lb, hb, eb):
    for s in range(PHYS):
        ab[s] = a_flat[s].reshape(NB, BS, BS)
    lb[:, :, BS:] = left[1].reshape(NB, BS, BS)
    env_part(left, at, env, ab, lb, hb, eb)


def sum_squares(ref, states):
    total = jnp.zeros((8, 128), F32)
    for s in range(states):
        for t in range(FLAT // 128):
            x = ref[s, :, t * 128 : (t + 1) * 128].astype(F32)
            x = x * x
            total = total + (x[0:8] + x[8:16]) + (x[16:24] + x[24:32])
    return total


def norm_factor(total):
    return lax.rsqrt(jnp.sum(total, keepdims=True) / (PHYS * NB * FLAT) + EPSILON)


def choose_kernel(tensor, new, low, high, out):
    odd = lax.rem(lax.axis_index("site"), 2) == 1
    first = jnp.logical_and(lax.axis_index("site") == 0, lax.axis_index("sec") == 0)

    @pl.when(odd)
    def _():
        out[...] = new[...]

    @pl.when(first)
    def _():
        out[...] = tensor[...]

    @pl.when(jnp.logical_not(jnp.logical_or(odd, first)))
    def _():
        factor = norm_factor(sum_squares(low, HALF) + sum_squares(high, HALF))
        for s in range(HALF):
            out[s] = scaled_copy(low[s], factor)
            out[HALF + s] = scaled_copy(high[s], factor)


def shape(*dims, dtype=BF16):
    return jax.ShapeDtypeStruct(dims, dtype)


def params(size):
    return pltpu.CompilerParams(vmem_limit_bytes=size * MIB)


def krylov(core_of, second, coupling, kept, *arrays):
    outs = [
        shape(ITERS + 1, PHYS, NB, BS, LN),
        shape(PHYS, NB, BS, LN, dtype=F32),
        shape(8, 128, dtype=F32),
        shape(NB, BS, PHYS * BS),
        shape(PHYS, NB, FLAT),
        shape(2, NB, FLAT),
    ]
    scratch = [
        pltpu.VMEM((PHYS, NB, FLAT), BF16),
        pltpu.VMEM((PHYS, NB, BS, BS), BF16),
        pltpu.VMEM((NB, BS, 2 * BS), BF16),
        pltpu.VMEM((NB, BS, BS), BF16),
        pltpu.VMEM((NB, BS, LN), BF16),
        pltpu.VMEM((NB, 2 * LN, LN), BF16),
        pltpu.SemaphoreType.DMA((4,)),
        pltpu.VMEM((2 * ITERS, 8, LN), F32),
        pltpu.VMEM((HALF, NB, FLAT), BF16),
        pltpu.VMEM((2, NB, FLAT), BF16),
        pltpu.VMEM((2, NB, BS, BS), BF16),
    ]
    if second:
        specs = [SM, SM] + [HB] * 6 + [VM]
    else:
        specs = [SM, SM] + [HB] * 6
    return pl.pallas_call(
        functools.partial(krylov_kernel, second, core_of),
        out_shape=tuple(outs),
        in_specs=specs,
        out_specs=(VM,) * len(outs),
        scratch_shapes=scratch,
        compiler_params=params(30),
        cost_estimate=pl.CostEstimate(flops=10**11, bytes_accessed=2**24, transcendentals=0),
        name="krylov",
    )(coupling, kept, *arrays)


def project(core_of, owner, own, got, u, last, at):
    return pl.pallas_call(
        functools.partial(project_kernel, owner, core_of),
        out_shape=shape(HALF, NB, FLAT),
        in_specs=[VM] * 5,
        out_specs=VM,
        scratch_shapes=[
            pltpu.VMEM((8, 128), F32),
            pltpu.VMEM((HALF, NB, BS, BS), BF16),
        ],
        compiler_params=params(20),
        cost_estimate=pl.CostEstimate(flops=10**6, bytes_accessed=2**10, transcendentals=0),
        name="project",
    )(own, got, u, last, at)


def grow(a_flat, left, at):
    return pl.pallas_call(
        env_kernel,
        out_shape=shape(2, NB, FLAT),
        in_specs=[VM] * 3,
        out_specs=VM,
        scratch_shapes=[
            pltpu.VMEM((PHYS, NB, BS, BS), BF16),
            pltpu.VMEM((NB, BS, 2 * BS), BF16),
            pltpu.VMEM((PHYS, NB, BS, 2 * BS), BF16),
            pltpu.VMEM((2, NB, BS, BS), BF16),
        ],
        compiler_params=params(12),
        cost_estimate=pl.CostEstimate(flops=10**6, bytes_accessed=2**10, transcendentals=0),
        name="grow",
    )(a_flat, left, at)


def choose(tensor, new, low, high):
    return pl.pallas_call(
        choose_kernel,
        out_shape=shape(PHYS, NB, FLAT),
        in_specs=[VM] * 4,
        out_specs=VM,
        compiler_params=params(8),
        name="choose",
    )(tensor, new, low, high)


def core_index():
    return lax.rem(lax.axis_index("site"), 2)


def shards(tensors, left_env, right_env, kept_rows, coupling):
    across = lax.axis_size("site")
    count = lax.axis_size("sec") * across
    position = lax.axis_index("sec") * across + lax.axis_index("site")
    axes = ("sec", "site")
    tensor, left, right = tensors[0], left_env[0], right_env[0]

    swap = [(i, i ^ 1) for i in range(count)]
    rise = [(i, i + 1) for i in range(0, count, 2)]
    fall = [(i + 1, i) for i in range(0, count, 2)]
    to_even = [(i, i - 2) for i in range(2, count, 2)]
    to_odd = [(i, i - 1) for i in range(2, count, 2)]
    from_even = [(i, i + 2) for i in range(0, count - 2, 2)]
    from_odd = [(i, i + 1) for i in range(1, count - 2, 2)]

    def send(x, pairs):
        return lax.ppermute(x, axes, pairs)

    got_t = send(tensor, swap)
    got_l = send(left, rise)
    got_r = send(right, fall)
    low, high, late_r, got_t, got_l, got_r = lax.optimization_barrier(
        (tensor[:HALF], tensor[HALF:], right, got_t, got_l, got_r)
    )
    b_even = send(low, to_even)
    b_odd = send(high, to_odd)
    r_even = send(late_r, to_even)
    r_odd = send(late_r, to_odd)

    u, last, small, at, a_flat, l_flat = krylov(
        core_index, False, coupling, kept_rows, tensor, got_t, left, got_l, right, got_r
    )
    got_small = send(small, swap)
    env1 = grow(a_flat, l_flat, at)
    x = project(core_index, 0, small, got_small, u, last, at)
    x, b_even, b_odd, r_even, r_odd = lax.optimization_barrier((x, b_even, b_odd, r_even, r_odd))
    got_x = send(x, swap)

    u, last, small, at, new1, env2 = krylov(
        core_index, True, coupling, kept_rows, x, got_x, b_even, b_odd, r_even, r_odd, env1
    )
    got_small = send(small, swap)
    x = project(core_index, 1, small, got_small, u, last, at)
    low = send(x, from_even)
    high = send(x, from_odd)
    got_env = send(env2, from_odd)

    odd = position % 2 == 1
    first = position == 0
    out_new = choose(tensor, new1, low, high)
    out_env = jnp.where(odd, env1, jnp.where(first, left, got_env))
    return out_new[None], out_env[None]


def solution(mesh):
    sites = P(("sec", "site"), None, None, None)
    return jax.shard_map(
        shards,
        mesh=mesh,
        in_specs=(sites, sites, sites, P(("sec", "site"), None), P()),
        out_specs=(sites, sites),
        check_vma=False,
    )
```

```python
import functools

import jax
import jax.numpy as jnp
from jax import lax
from jax.experimental import pallas as pl
from jax.experimental.pallas import tpu as pltpu
from jax.sharding import PartitionSpec as P

NN = 8
NS = 4
BS = 64
PHYS = 4
ITERS = 4
NB = 32
FLAT = BS * BS
CHARGE_NUMBER = (0, 1, 1, 2)
CHARGE_SPIN = (0, 1, -1, 0)
OCCUPANCY = (0.0, 1.0, 1.0, 2.0)
STEP_SIZE = 0.06
EPSILON = 1e-06
HALF = PHYS // 2
LN = HALF * BS
F32, BF16 = jnp.float32, jnp.bfloat16
MIB = 2**20
VM = pl.BlockSpec(memory_space=pltpu.VMEM)
SM = pl.BlockSpec(memory_space=pltpu.SMEM)
HB = pl.BlockSpec(memory_space=pltpu.HBM)


def dot(a, b):
    return jnp.dot(a, b, preferred_element_type=F32)


def sector(q, number, spin):
    return (q // NS + number) % NN * NS + (q % NS + spin) % NS


def plus(q, s):
    return sector(q, CHARGE_NUMBER[s], CHARGE_SPIN[s])


def minus(q, s):
    return sector(q, -CHARGE_NUMBER[s], -CHARGE_SPIN[s])


def fold(x):
    total = x[0:8]
    for i in range(1, BS // 8):
        total = total + x[i * 8 : (i + 1) * 8]
    return total


def scaled_copy(src, factor):
    return (src.astype(F32) * factor).astype(BF16)


def krylov_kernel(second, core_of, *refs):
    if second:
        coup, kept, a_raw, b_even, b_odd, r_even, r_odd, left_raw = refs[:8]
        outs = refs[8:11]
        scratch = refs[11:]
    else:
        coup, kept, own, got, own_l, got_l, own_r, got_r = refs[:8]
        outs = refs[8:14]
        scratch = refs[14:]
    u, last, small = outs[:3]
    ab, lb, rb, bcat, w, sems, moments, b_raw, r_raw = scratch[:9]
    y = last
    core = core_of()

    if not second:
        at, a_flat, left_raw = outs[3:]
        a_raw = scratch[9]

    def moves(odd):
        if second:
            pairs = [
                (b_odd if odd else b_even, b_raw),
                (r_odd if odd else r_even, r_raw),
            ]
        else:
            t_a, t_b = (got, own) if odd else (own, got)
            pairs = [
                (t_a, a_raw),
                (t_b.at[pl.ds(HALF if odd else 0, HALF)], b_raw),
                (got_l if odd else own_l, left_raw),
                (own_r if odd else got_r, r_raw),
            ]
        return [pltpu.make_async_copy(x, z, sems.at[i]) for i, (x, z) in enumerate(pairs)]

    for odd in (False, True):

        @pl.when(core == int(odd))
        def _(odd=odd):
            for copy in moves(odd):
                copy.start()
            for copy in moves(odd):
                copy.wait()

    lane = lax.broadcasted_iota(jnp.int32, (1, LN), 1)
    rows16 = [
        jnp.where(lane < BS, coup[s1, core * HALF], coup[s1, core * HALF + 1]).astype(BF16)
        for s1 in range(PHYS)
    ]

    for ch in range(2):
        rb[...] = r_raw[ch].reshape(NB, BS, BS)
        for q in range(NB):
            for h in range(HALF):
                low, high = plus(q, h), plus(q, HALF + h)
                block = rb[low + core * (high - low)]
                zero = jnp.zeros((BS, BS), BF16)
                parts = [block, zero] if h == 0 else [zero, block]
                w[q, ch * LN + h * BS : ch * LN + (h + 1) * BS] = jnp.concatenate(parts, 1)
    for ch in range(2):
        lb[:, :, ch * BS : (ch + 1) * BS] = left_raw[ch].reshape(NB, BS, BS)
    for h in range(HALF):
        bcat[:, :, h * BS : (h + 1) * BS] = b_raw[h].reshape(NB, BS, BS)

    for s in range(PHYS):
        x = a_raw[s]
        if not second:
            a_flat[s] = x
        ab[s] = x.reshape(NB, BS, BS)

    for q in range(NB):
        if not second:
            for s1 in range(PHYS):
                at[q, :, s1 * BS : (s1 + 1) * BS] = ab[s1, minus(q, s1)].T
        lhs = jnp.concatenate([ab[s1, minus(q, s1)] for s1 in range(PHYS)], 0)
        out = dot(lhs, bcat[q]).astype(BF16)
        for s1 in range(PHYS):
            u[0, s1, minus(q, s1)] = out[s1 * BS : (s1 + 1) * BS]

    def product(it, _):
        now, later = u.at[it], u.at[it + 1]
        for q in range(NB):
            x = jnp.concatenate([now[s1, minus(q, s1)] for s1 in range(PHYS)], 0)
            c = jnp.concatenate([now[s1, minus(q, s1)] * rows16[s1] for s1 in range(PHYS)], 0)
            out = dot(jnp.concatenate([x, c], 1), w[q])
            for s1 in range(PHYS):
                y[s1, minus(q, s1)] = out[s1 * BS : (s1 + 1) * BS]
        even = jnp.zeros((8, LN), F32)
        odd = jnp.zeros((8, LN), F32)
        for q in range(NB):
            for pair in range(PHYS // 2):
                xs = [now[pair * 2 + j, q] for j in range(2)]
                cs = [xs[j] * rows16[pair * 2 + j] for j in range(2)]
                rhs = jnp.concatenate([jnp.concatenate(xs, 1), jnp.concatenate(cs, 1)], 0)
                out = dot(lb[q], rhs)
                for j in range(2):
                    s1 = pair * 2 + j
                    old = xs[j].astype(F32)
                    new = old - STEP_SIZE * (out[:, j * LN : (j + 1) * LN] + y[s1, q])
                    y[s1, q] = new
                    later[s1, q] = new.astype(BF16)
                    even = even + fold(old * old)
                    odd = odd + fold(old * new)
        moments[2 * it] = even
        moments[2 * it + 1] = odd
        return 0

    lax.fori_loop(0, ITERS, product, 0)

    row = lax.broadcasted_iota(jnp.int32, (8, 128), 0)
    column = lax.broadcasted_iota(jnp.int32, (8, 128), 1)
    out = jnp.zeros((8, 128), F32)
    for k in range(2 * ITERS):
        out = jnp.where((row == 0) & (column == k), jnp.sum(moments[k], keepdims=True), out)
    for q in range(NB):
        out = jnp.where((row == 1) & (column == q), kept[0, q].astype(F32), out)
    small[...] = out


def project_kernel(owner, core_of, own, got, u, last, at, x_out, v, xb):
    core = core_of()
    mine, other = own[...], got[...]
    both = mine + other
    row = lax.broadcasted_iota(jnp.int32, (8, 128), 0)
    column = lax.broadcasted_iota(jnp.int32, (8, 128), 1)

    def entry(array, r, c):
        return jnp.sum(jnp.where((row == r) & (column == c), array, 0.0), keepdims=True)

    t = [entry(both, 0, k) for k in range(2 * ITERS)]
    a = [jnp.ones((1, 1), F32)]
    for it in range(ITERS):
        den = sum(a[k] * a[j] * t[k + j] for k in range(it + 1) for j in range(it + 1))
        num = sum(a[k] * a[j] * t[k + j + 1] for k in range(it + 1) for j in range(it + 1))
        delta = 1.0 - num / den
        a = (
            [delta * a[0]]
            + [a[k - 1] + delta * a[k] for k in range(1, it + 1)]
            + [a[it]]
        )
    kept = jnp.where(core == owner, mine, other)
    row_ids = lax.broadcasted_iota(jnp.int32, (BS, LN), 0).astype(F32)
    for p in range(NB):
        parts = []
        for s1 in range(PHYS):
            q = minus(p, s1)
            total = last[s1, q]
            for k in range(ITERS):
                total = total + a[k] * u[k, s1, q].astype(F32)
            parts.append(total.astype(BF16))
        out = dot(at[p], jnp.concatenate(parts, 0))
        out = jnp.where(row_ids < entry(kept, 1, p), out, 0.0).astype(BF16)
        for h in range(HALF):
            xb[h, p] = out[:, h * BS : (h + 1) * BS]
    for h in range(HALF):
        x_out[h] = xb[h].reshape(NB, FLAT)


def env_part(left, at, env, ab, lb, hb, eb):
    mixed = (left[0].astype(F32) + left[1].astype(F32)).astype(BF16)
    lb[:, :, :BS] = mixed.reshape(NB, BS, BS)
    for q in range(NB):
        lhs = jnp.concatenate(
            [at[plus(q, s), :, s * BS : (s + 1) * BS] for s in range(PHYS)], 0
        )
        out = dot(lhs, lb[q]).astype(BF16)
        for s in range(PHYS):
            hb[s, q] = out[s * BS : (s + 1) * BS]
    for p in range(NB):
        halves = [hb[s, minus(p, s)] for s in range(PHYS)]
        energy = jnp.concatenate([half[:, :BS] for half in halves], 1)
        density = jnp.concatenate(
            [half[:, BS:] * BF16(OCCUPANCY[s]) for s, half in enumerate(halves)], 1
        )
        stack = jnp.concatenate([ab[s, minus(p, s)] for s in range(PHYS)], 0)
        out = dot(jnp.concatenate([energy, density], 0), stack) * (1.0 / (PHYS * BS))
        out = out.astype(BF16)
        eb[0, p] = out[:BS]
        eb[1, p] = out[BS:]
    for ch in range(2):
        env[ch] = eb[ch].reshape(NB, FLAT)


def env_kernel(a_flat, left, at, env, ab, lb, hb, eb):
    for s in range(PHYS):
        ab[s] = a_flat[s].reshape(NB, BS, BS)
    lb[:, :, BS:] = left[1].reshape(NB, BS, BS)
    env_part(left, at, env, ab, lb, hb, eb)


def sum_squares(ref, states):
    total = jnp.zeros((8, 128), F32)
    for s in range(states):
        for t in range(FLAT // 128):
            x = ref[s, :, t * 128 : (t + 1) * 128].astype(F32)
            x = x * x
            total = total + (x[0:8] + x[8:16]) + (x[16:24] + x[24:32])
    return total


def norm_factor(total):
    return lax.rsqrt(jnp.sum(total, keepdims=True) / (PHYS * NB * FLAT) + EPSILON)


def prepare_kernel(core_of, own, got, left, new, at, env, ab, lb, hb, eb):
    core = core_of()
    factor = norm_factor(sum_squares(own, HALF) + sum_squares(got, HALF))
    for h in range(HALF):
        new[core * HALF + h] = scaled_copy(own[h], factor)
        new[(1 - core) * HALF + h] = scaled_copy(got[h], factor)
    for s in range(PHYS):
        ab[s] = new[s].reshape(NB, BS, BS)
    for q in range(NB):
        for s1 in range(PHYS):
            at[q, :, s1 * BS : (s1 + 1) * BS] = ab[s1, minus(q, s1)].T
    lb[:, :, BS:] = left[1].reshape(NB, BS, BS)
    env_part(left, at, env, ab, lb, hb, eb)


def choose_kernel(tensor, new, low, high, out):
    odd = lax.rem(lax.axis_index("site"), 2) == 1
    first = jnp.logical_and(lax.axis_index("site") == 0, lax.axis_index("sec") == 0)

    @pl.when(odd)
    def _():
        out[...] = new[...]

    @pl.when(first)
    def _():
        out[...] = tensor[...]

    @pl.when(jnp.logical_not(jnp.logical_or(odd, first)))
    def _():
        factor = norm_factor(sum_squares(low, HALF) + sum_squares(high, HALF))
        for s in range(HALF):
            out[s] = scaled_copy(low[s], factor)
            out[HALF + s] = scaled_copy(high[s], factor)


def shape(*dims, dtype=BF16):
    return jax.ShapeDtypeStruct(dims, dtype)


def params(size):
    return pltpu.CompilerParams(vmem_limit_bytes=size * MIB)


def krylov(core_of, second, coupling, kept, *arrays):
    outs = [
        shape(ITERS + 1, PHYS, NB, BS, LN),
        shape(PHYS, NB, BS, LN, dtype=F32),
        shape(8, 128, dtype=F32),
    ]
    if not second:
        outs += [shape(NB, BS, PHYS * BS), shape(PHYS, NB, FLAT), shape(2, NB, FLAT)]
    scratch = [
        pltpu.VMEM((PHYS, NB, BS, BS), BF16),
        pltpu.VMEM((NB, BS, 2 * BS), BF16),
        pltpu.VMEM((NB, BS, BS), BF16),
        pltpu.VMEM((NB, BS, LN), BF16),
        pltpu.VMEM((NB, 2 * LN, LN), BF16),
        pltpu.SemaphoreType.DMA((4,)),
        pltpu.VMEM((2 * ITERS, 8, LN), F32),
        pltpu.VMEM((HALF, NB, FLAT), BF16),
        pltpu.VMEM((2, NB, FLAT), BF16),
    ]
    if second:
        specs = [SM, SM, VM] + [HB] * 4 + [VM]
    else:
        specs = [SM, SM] + [HB] * 6
        scratch.append(pltpu.VMEM((PHYS, NB, FLAT), BF16))
    return pl.pallas_call(
        functools.partial(krylov_kernel, second, core_of),
        out_shape=tuple(outs),
        in_specs=specs,
        out_specs=(VM,) * len(outs),
        scratch_shapes=scratch,
        compiler_params=params(28),
        cost_estimate=pl.CostEstimate(flops=10**11, bytes_accessed=2**24, transcendentals=0),
        name="krylov",
    )(coupling, kept, *arrays)


def project(core_of, owner, own, got, u, last, at):
    return pl.pallas_call(
        functools.partial(project_kernel, owner, core_of),
        out_shape=shape(HALF, NB, FLAT),
        in_specs=[VM] * 5,
        out_specs=VM,
        scratch_shapes=[
            pltpu.VMEM((8, 128), F32),
            pltpu.VMEM((HALF, NB, BS, BS), BF16),
        ],
        compiler_params=params(20),
        cost_estimate=pl.CostEstimate(flops=10**6, bytes_accessed=2**10, transcendentals=0),
        name="project",
    )(own, got, u, last, at)


def grow(a_flat, left, at):
    return pl.pallas_call(
        env_kernel,
        out_shape=shape(2, NB, FLAT),
        in_specs=[VM] * 3,
        out_specs=VM,
        scratch_shapes=[
            pltpu.VMEM((PHYS, NB, BS, BS), BF16),
            pltpu.VMEM((NB, BS, 2 * BS), BF16),
            pltpu.VMEM((PHYS, NB, BS, 2 * BS), BF16),
            pltpu.VMEM((2, NB, BS, BS), BF16),
        ],
        compiler_params=params(12),
        cost_estimate=pl.CostEstimate(flops=10**6, bytes_accessed=2**10, transcendentals=0),
        name="grow",
    )(a_flat, left, at)


def prepare(core_of, own, got, left):
    return pl.pallas_call(
        functools.partial(prepare_kernel, core_of),
        out_shape=(
            shape(PHYS, NB, FLAT),
            shape(NB, BS, PHYS * BS),
            shape(2, NB, FLAT),
        ),
        in_specs=[VM] * 3,
        out_specs=(VM,) * 3,
        scratch_shapes=[
            pltpu.VMEM((PHYS, NB, BS, BS), BF16),
            pltpu.VMEM((NB, BS, 2 * BS), BF16),
            pltpu.VMEM((PHYS, NB, BS, 2 * BS), BF16),
            pltpu.VMEM((2, NB, BS, BS), BF16),
        ],
        compiler_params=params(12),
        cost_estimate=pl.CostEstimate(flops=10**6, bytes_accessed=2**10, transcendentals=0),
        name="prepare",
    )(own, got, left)


def choose(tensor, new, low, high):
    return pl.pallas_call(
        choose_kernel,
        out_shape=shape(PHYS, NB, FLAT),
        in_specs=[VM] * 4,
        out_specs=VM,
        compiler_params=params(8),
        name="choose",
    )(tensor, new, low, high)


def core_index():
    return lax.rem(lax.axis_index("site"), 2)


def shards(tensors, left_env, right_env, kept_rows, coupling):
    across = lax.axis_size("site")
    count = lax.axis_size("sec") * across
    position = lax.axis_index("sec") * across + lax.axis_index("site")
    axes = ("sec", "site")
    tensor, left, right = tensors[0], left_env[0], right_env[0]

    swap = [(i, i ^ 1) for i in range(count)]
    rise = [(i, i + 1) for i in range(0, count, 2)]
    fall = [(i + 1, i) for i in range(0, count, 2)]
    to_even = [(i, i - 2) for i in range(2, count, 2)]
    to_odd = [(i, i - 1) for i in range(2, count, 2)]
    from_even = [(i, i + 2) for i in range(0, count - 2, 2)]
    from_odd = [(i, i + 1) for i in range(1, count - 2, 2)]

    def send(x, pairs):
        return lax.ppermute(x, axes, pairs)

    got_t = send(tensor, swap)
    got_l = send(left, rise)
    got_r = send(right, fall)
    low, high, late_r, got_t, got_l, got_r = lax.optimization_barrier(
        (tensor[:HALF], tensor[HALF:], right, got_t, got_l, got_r)
    )
    b_even = send(low, to_even)
    b_odd = send(high, to_odd)
    r_even = send(late_r, to_even)
    r_odd = send(late_r, to_odd)

    u, last, small, at, a_flat, l_flat = krylov(
        core_index, False, coupling, kept_rows, tensor, got_t, left, got_l, right, got_r
    )
    got_small = send(small, swap)
    env1 = grow(a_flat, l_flat, at)
    x = project(core_index, 0, small, got_small, u, last, at)
    x, b_even, b_odd, r_even, r_odd = lax.optimization_barrier((x, b_even, b_odd, r_even, r_odd))
    got_x = send(x, swap)

    new1, at, env2 = prepare(core_index, x, got_x, env1)
    got_env = send(env2, from_odd)
    u, last, small = krylov(
        core_index, True, coupling, kept_rows, new1, b_even, b_odd, r_even, r_odd, env1
    )
    got_small = send(small, swap)
    x = project(core_index, 1, small, got_small, u, last, at)
    low = send(x, from_even)
    high = send(x, from_odd)
    got_env, low, high = lax.optimization_barrier((got_env, low, high))

    odd = position % 2 == 1
    first = position == 0
    out_new = choose(tensor, new1, low, high)
    out_env = jnp.where(odd, env1, jnp.where(first, left, got_env))
    return out_new[None], out_env[None]


def solution(mesh):
    sites = P(("sec", "site"), None, None, None)
    return jax.shard_map(
        shards,
        mesh=mesh,
        in_specs=(sites, sites, sites, P(("sec", "site"), None), P()),
        out_specs=(sites, sites),
        check_vma=False,
    )
```

```python
import functools

import jax
import jax.numpy as jnp
from jax import lax
from jax.experimental import pallas as pl
from jax.experimental.pallas import tpu as pltpu
from jax.sharding import PartitionSpec as P

NN = 8
NS = 4
BS = 64
PHYS = 4
ITERS = 4
NB = 32
FLAT = BS * BS
CHARGE_NUMBER = (0, 1, 1, 2)
CHARGE_SPIN = (0, 1, -1, 0)
OCCUPANCY = (0.0, 1.0, 1.0, 2.0)
STEP_SIZE = 0.06
EPSILON = 1e-06
HALF = PHYS // 2
LN = HALF * BS
F32, BF16 = jnp.float32, jnp.bfloat16
MIB = 2**20
VM = pl.BlockSpec(memory_space=pltpu.VMEM)
SM = pl.BlockSpec(memory_space=pltpu.SMEM)
HB = pl.BlockSpec(memory_space=pltpu.HBM)


def dot(a, b):
    return jnp.dot(a, b, preferred_element_type=F32)


def sector(q, number, spin):
    return (q // NS + number) % NN * NS + (q % NS + spin) % NS


def plus(q, s):
    return sector(q, CHARGE_NUMBER[s], CHARGE_SPIN[s])


def minus(q, s):
    return sector(q, -CHARGE_NUMBER[s], -CHARGE_SPIN[s])


def fold(x):
    total = x[0:8]
    for i in range(1, BS // 8):
        total = total + x[i * 8 : (i + 1) * 8]
    return total


def scaled_copy(src, factor):
    return (src.astype(F32) * factor).astype(BF16)


def krylov_kernel(second, core_of, *refs):
    if second:
        coup, kept, a_raw, b_even, b_odd, r_even, r_odd, left_raw = refs[:8]
        outs = refs[8:11]
        scratch = refs[11:]
    else:
        coup, kept, own, got, own_l, got_l, own_r, got_r = refs[:8]
        outs = refs[8:14]
        scratch = refs[14:]
    u, last, small = outs[:3]
    ab, lb, rb, bcat, w, sems, moments, b_raw, r_raw = scratch[:9]
    y = last
    core = core_of()

    if not second:
        at, a_flat, left_raw = outs[3:]
        a_raw = scratch[9]

    def moves(odd):
        if second:
            pairs = [
                (b_odd if odd else b_even, b_raw),
                (r_odd if odd else r_even, r_raw),
            ]
        else:
            t_a, t_b = (got, own) if odd else (own, got)
            pairs = [
                (t_a, a_raw),
                (t_b.at[pl.ds(HALF if odd else 0, HALF)], b_raw),
                (got_l if odd else own_l, left_raw),
                (own_r if odd else got_r, r_raw),
            ]
        return [pltpu.make_async_copy(x, z, sems.at[i]) for i, (x, z) in enumerate(pairs)]

    for odd in (False, True):

        @pl.when(core == int(odd))
        def _(odd=odd):
            for copy in moves(odd):
                copy.start()
            for copy in moves(odd):
                copy.wait()

    lane = lax.broadcasted_iota(jnp.int32, (1, LN), 1)
    rows16 = [
        jnp.where(lane < BS, coup[s1, core * HALF], coup[s1, core * HALF + 1]).astype(BF16)
        for s1 in range(PHYS)
    ]

    for ch in range(2):
        rb[...] = r_raw[ch].reshape(NB, BS, BS)
        for q in range(NB):
            for h in range(HALF):
                low, high = plus(q, h), plus(q, HALF + h)
                block = rb[low + core * (high - low)]
                zero = jnp.zeros((BS, BS), BF16)
                parts = [block, zero] if h == 0 else [zero, block]
                w[q, ch * LN + h * BS : ch * LN + (h + 1) * BS] = jnp.concatenate(parts, 1)
    for ch in range(2):
        lb[:, :, ch * BS : (ch + 1) * BS] = left_raw[ch].reshape(NB, BS, BS)
    for h in range(HALF):
        bcat[:, :, h * BS : (h + 1) * BS] = b_raw[h].reshape(NB, BS, BS)

    for s in range(PHYS):
        x = a_raw[s]
        if not second:
            a_flat[s] = x
        ab[s] = x.reshape(NB, BS, BS)

    for q in range(NB):
        if not second:
            for s1 in range(PHYS):
                at[q, :, s1 * BS : (s1 + 1) * BS] = ab[s1, minus(q, s1)].T
        lhs = jnp.concatenate([ab[s1, minus(q, s1)] for s1 in range(PHYS)], 0)
        out = dot(lhs, bcat[q]).astype(BF16)
        for s1 in range(PHYS):
            u[0, s1, minus(q, s1)] = out[s1 * BS : (s1 + 1) * BS]

    def product(it, _):
        now, later = u.at[it], u.at[it + 1]
        for q in range(NB):
            x = jnp.concatenate([now[s1, minus(q, s1)] for s1 in range(PHYS)], 0)
            c = jnp.concatenate([now[s1, minus(q, s1)] * rows16[s1] for s1 in range(PHYS)], 0)
            out = dot(jnp.concatenate([x, c], 1), w[q])
            for s1 in range(PHYS):
                y[s1, minus(q, s1)] = out[s1 * BS : (s1 + 1) * BS]
        even = jnp.zeros((8, LN), F32)
        odd = jnp.zeros((8, LN), F32)
        for q in range(NB):
            for pair in range(PHYS // 2):
                xs = [now[pair * 2 + j, q] for j in range(2)]
                cs = [xs[j] * rows16[pair * 2 + j] for j in range(2)]
                rhs = jnp.concatenate([jnp.concatenate(xs, 1), jnp.concatenate(cs, 1)], 0)
                out = dot(lb[q], rhs)
                for j in range(2):
                    s1 = pair * 2 + j
                    old = xs[j].astype(F32)
                    new = old - STEP_SIZE * (out[:, j * LN : (j + 1) * LN] + y[s1, q])
                    y[s1, q] = new
                    later[s1, q] = new.astype(BF16)
                    even = even + fold(old * old)
                    odd = odd + fold(old * new)
        moments[2 * it] = even
        moments[2 * it + 1] = odd
        return 0

    lax.fori_loop(0, ITERS, product, 0)

    row = lax.broadcasted_iota(jnp.int32, (8, 128), 0)
    column = lax.broadcasted_iota(jnp.int32, (8, 128), 1)
    out = jnp.zeros((8, 128), F32)
    for k in range(2 * ITERS):
        out = jnp.where((row == 0) & (column == k), jnp.sum(moments[k], keepdims=True), out)
    for q in range(NB):
        out = jnp.where((row == 1) & (column == q), kept[0, q].astype(F32), out)
    small[...] = out


def project_kernel(owner, core_of, own, got, u, last, at, x_out, v, xb):
    core = core_of()
    mine, other = own[...], got[...]
    both = mine + other
    row = lax.broadcasted_iota(jnp.int32, (8, 128), 0)
    column = lax.broadcasted_iota(jnp.int32, (8, 128), 1)

    def entry(array, r, c):
        return jnp.sum(jnp.where((row == r) & (column == c), array, 0.0), keepdims=True)

    t = [entry(both, 0, k) for k in range(2 * ITERS)]
    a = [jnp.ones((1, 1), F32)]
    for it in range(ITERS):
        den = sum(a[k] * a[j] * t[k + j] for k in range(it + 1) for j in range(it + 1))
        num = sum(a[k] * a[j] * t[k + j + 1] for k in range(it + 1) for j in range(it + 1))
        delta = 1.0 - num / den
        a = (
            [delta * a[0]]
            + [a[k - 1] + delta * a[k] for k in range(1, it + 1)]
            + [a[it]]
        )
    kept = jnp.where(core == owner, mine, other)
    row_ids = lax.broadcasted_iota(jnp.int32, (BS, LN), 0).astype(F32)
    for p in range(NB):
        parts = []
        for s1 in range(PHYS):
            q = minus(p, s1)
            total = last[s1, q]
            for k in range(ITERS):
                total = total + a[k] * u[k, s1, q].astype(F32)
            parts.append(total.astype(BF16))
        out = dot(at[p], jnp.concatenate(parts, 0))
        out = jnp.where(row_ids < entry(kept, 1, p), out, 0.0).astype(BF16)
        for h in range(HALF):
            xb[h, p] = out[:, h * BS : (h + 1) * BS]
    for h in range(HALF):
        x_out[h] = xb[h].reshape(NB, FLAT)


def env_part(left, at, env, ab, lb, hb, eb):
    mixed = (left[0].astype(F32) + left[1].astype(F32)).astype(BF16)
    lb[:, :, :BS] = mixed.reshape(NB, BS, BS)
    for q in range(NB):
        lhs = jnp.concatenate(
            [at[plus(q, s), :, s * BS : (s + 1) * BS] for s in range(PHYS)], 0
        )
        out = dot(lhs, lb[q]).astype(BF16)
        for s in range(PHYS):
            hb[s, q] = out[s * BS : (s + 1) * BS]
    for p in range(NB):
        halves = [hb[s, minus(p, s)] for s in range(PHYS)]
        energy = jnp.concatenate([half[:, :BS] for half in halves], 1)
        density = jnp.concatenate(
            [half[:, BS:] * BF16(OCCUPANCY[s]) for s, half in enumerate(halves)], 1
        )
        stack = jnp.concatenate([ab[s, minus(p, s)] for s in range(PHYS)], 0)
        out = dot(jnp.concatenate([energy, density], 0), stack) * (1.0 / (PHYS * BS))
        out = out.astype(BF16)
        eb[0, p] = out[:BS]
        eb[1, p] = out[BS:]
    for ch in range(2):
        env[ch] = eb[ch].reshape(NB, FLAT)


def env_kernel(a_flat, left, at, env, ab, lb, hb, eb):
    for s in range(PHYS):
        ab[s] = a_flat[s].reshape(NB, BS, BS)
    lb[:, :, BS:] = left[1].reshape(NB, BS, BS)
    env_part(left, at, env, ab, lb, hb, eb)


def sum_squares(ref, states):
    total = jnp.zeros((8, 128), F32)
    for s in range(states):
        for t in range(FLAT // 128):
            x = ref[s, :, t * 128 : (t + 1) * 128].astype(F32)
            x = x * x
            total = total + (x[0:8] + x[8:16]) + (x[16:24] + x[24:32])
    return total


def norm_factor(total):
    return lax.rsqrt(jnp.sum(total, keepdims=True) / (PHYS * NB * FLAT) + EPSILON)


def prepare_kernel(core_of, own, got, left, new, at, env, ab, lb, hb, eb):
    core = core_of()
    factor = norm_factor(sum_squares(own, HALF) + sum_squares(got, HALF))
    for h in range(HALF):
        new[core * HALF + h] = scaled_copy(own[h], factor)
        new[(1 - core) * HALF + h] = scaled_copy(got[h], factor)
    for s in range(PHYS):
        ab[s] = new[s].reshape(NB, BS, BS)
    for q in range(NB):
        for s1 in range(PHYS):
            at[q, :, s1 * BS : (s1 + 1) * BS] = ab[s1, minus(q, s1)].T
    lb[:, :, BS:] = left[1].reshape(NB, BS, BS)
    env_part(left, at, env, ab, lb, hb, eb)


def choose_kernel(tensor, new, low, high, left, env, got_env, out, out_env):
    odd = lax.rem(lax.axis_index("site"), 2) == 1
    first = jnp.logical_and(lax.axis_index("site") == 0, lax.axis_index("sec") == 0)

    @pl.when(odd)
    def _():
        out[...] = new[...]
        out_env[...] = env[...]

    @pl.when(first)
    def _():
        out[...] = tensor[...]
        out_env[...] = left[...]

    @pl.when(jnp.logical_not(jnp.logical_or(odd, first)))
    def _():
        factor = norm_factor(sum_squares(low, HALF) + sum_squares(high, HALF))
        for s in range(HALF):
            out[s] = scaled_copy(low[s], factor)
            out[HALF + s] = scaled_copy(high[s], factor)
        out_env[...] = got_env[...]


def shape(*dims, dtype=BF16):
    return jax.ShapeDtypeStruct(dims, dtype)


def params(size):
    return pltpu.CompilerParams(vmem_limit_bytes=size * MIB)


def krylov(core_of, second, coupling, kept, *arrays):
    outs = [
        shape(ITERS + 1, PHYS, NB, BS, LN),
        shape(PHYS, NB, BS, LN, dtype=F32),
        shape(8, 128, dtype=F32),
    ]
    if not second:
        outs += [shape(NB, BS, PHYS * BS), shape(PHYS, NB, FLAT), shape(2, NB, FLAT)]
    scratch = [
        pltpu.VMEM((PHYS, NB, BS, BS), BF16),
        pltpu.VMEM((NB, BS, 2 * BS), BF16),
        pltpu.VMEM((NB, BS, BS), BF16),
        pltpu.VMEM((NB, BS, LN), BF16),
        pltpu.VMEM((NB, 2 * LN, LN), BF16),
        pltpu.SemaphoreType.DMA((4,)),
        pltpu.VMEM((2 * ITERS, 8, LN), F32),
        pltpu.VMEM((HALF, NB, FLAT), BF16),
        pltpu.VMEM((2, NB, FLAT), BF16),
    ]
    if second:
        specs = [SM, SM, VM] + [HB] * 4 + [VM]
    else:
        specs = [SM, SM] + [HB] * 6
        scratch.append(pltpu.VMEM((PHYS, NB, FLAT), BF16))
    return pl.pallas_call(
        functools.partial(krylov_kernel, second, core_of),
        out_shape=tuple(outs),
        in_specs=specs,
        out_specs=(VM,) * len(outs),
        scratch_shapes=scratch,
        compiler_params=params(28),
        cost_estimate=pl.CostEstimate(flops=10**11, bytes_accessed=2**24, transcendentals=0),
        name="krylov",
    )(coupling, kept, *arrays)


def project(core_of, owner, own, got, u, last, at):
    return pl.pallas_call(
        functools.partial(project_kernel, owner, core_of),
        out_shape=shape(HALF, NB, FLAT),
        in_specs=[VM] * 5,
        out_specs=VM,
        scratch_shapes=[
            pltpu.VMEM((8, 128), F32),
            pltpu.VMEM((HALF, NB, BS, BS), BF16),
        ],
        compiler_params=params(20),
        cost_estimate=pl.CostEstimate(flops=10**6, bytes_accessed=2**10, transcendentals=0),
        name="project",
    )(own, got, u, last, at)


def grow(a_flat, left, at):
    return pl.pallas_call(
        env_kernel,
        out_shape=shape(2, NB, FLAT),
        in_specs=[VM] * 3,
        out_specs=VM,
        scratch_shapes=[
            pltpu.VMEM((PHYS, NB, BS, BS), BF16),
            pltpu.VMEM((NB, BS, 2 * BS), BF16),
            pltpu.VMEM((PHYS, NB, BS, 2 * BS), BF16),
            pltpu.VMEM((2, NB, BS, BS), BF16),
        ],
        compiler_params=params(12),
        cost_estimate=pl.CostEstimate(flops=10**6, bytes_accessed=2**10, transcendentals=0),
        name="grow",
    )(a_flat, left, at)


def prepare(core_of, own, got, left):
    return pl.pallas_call(
        functools.partial(prepare_kernel, core_of),
        out_shape=(
            shape(PHYS, NB, FLAT),
            shape(NB, BS, PHYS * BS),
            shape(2, NB, FLAT),
        ),
        in_specs=[VM] * 3,
        out_specs=(VM,) * 3,
        scratch_shapes=[
            pltpu.VMEM((PHYS, NB, BS, BS), BF16),
            pltpu.VMEM((NB, BS, 2 * BS), BF16),
            pltpu.VMEM((PHYS, NB, BS, 2 * BS), BF16),
            pltpu.VMEM((2, NB, BS, BS), BF16),
        ],
        compiler_params=params(12),
        cost_estimate=pl.CostEstimate(flops=10**6, bytes_accessed=2**10, transcendentals=0),
        name="prepare",
    )(own, got, left)


def choose(*arrays):
    return pl.pallas_call(
        choose_kernel,
        out_shape=(shape(PHYS, NB, FLAT), shape(2, NB, FLAT)),
        in_specs=[VM] * 7,
        out_specs=(VM, VM),
        compiler_params=params(12),
        name="choose",
    )(*arrays)


def core_index():
    return lax.rem(lax.axis_index("site"), 2)


def shards(tensors, left_env, right_env, kept_rows, coupling):
    across = lax.axis_size("site")
    count = lax.axis_size("sec") * across
    axes = ("sec", "site")
    tensor, left, right = tensors[0], left_env[0], right_env[0]

    swap = [(i, i ^ 1) for i in range(count)]
    rise = [(i, i + 1) for i in range(0, count, 2)]
    fall = [(i + 1, i) for i in range(0, count, 2)]
    to_even = [(i, i - 2) for i in range(2, count, 2)]
    to_odd = [(i, i - 1) for i in range(2, count, 2)]
    from_even = [(i, i + 2) for i in range(0, count - 2, 2)]
    from_odd = [(i, i + 1) for i in range(1, count - 2, 2)]

    def send(x, pairs):
        return lax.ppermute(x, axes, pairs)

    got_t = send(tensor, swap)
    got_l = send(left, rise)
    got_r = send(right, fall)
    low, high, late_r, got_t, got_l, got_r = lax.optimization_barrier(
        (tensor[:HALF], tensor[HALF:], right, got_t, got_l, got_r)
    )
    b_even = send(low, to_even)
    b_odd = send(high, to_odd)
    r_even = send(late_r, to_even)
    r_odd = send(late_r, to_odd)

    u, last, small, at, a_flat, l_flat = krylov(
        core_index, False, coupling, kept_rows, tensor, got_t, left, got_l, right, got_r
    )
    got_small = send(small, swap)
    env1 = grow(a_flat, l_flat, at)
    x = project(core_index, 0, small, got_small, u, last, at)
    x, b_even, b_odd, r_even, r_odd = lax.optimization_barrier((x, b_even, b_odd, r_even, r_odd))
    got_x = send(x, swap)

    new1, at, env2 = prepare(core_index, x, got_x, env1)
    got_env = send(env2, from_odd)
    u, last, small = krylov(
        core_index, True, coupling, kept_rows, new1, b_even, b_odd, r_even, r_odd, env1
    )
    got_small = send(small, swap)
    x = project(core_index, 1, small, got_small, u, last, at)
    x, got_env = lax.optimization_barrier((x, got_env))
    low = send(x, from_even)
    high = send(x, from_odd)
    got_env, low, high = lax.optimization_barrier((got_env, low, high))

    out_new, out_env = choose(tensor, new1, low, high, left, env1, got_env)
    return out_new[None], out_env[None]


def solution(mesh):
    sites = P(("sec", "site"), None, None, None)
    return jax.shard_map(
        shards,
        mesh=mesh,
        in_specs=(sites, sites, sites, P(("sec", "site"), None), P()),
        out_specs=(sites, sites),
        check_vma=False,
    )
```

```python
import functools

import jax
import jax.numpy as jnp
from jax import lax
from jax.experimental import pallas as pl
from jax.experimental.pallas import tpu as pltpu
from jax.sharding import PartitionSpec as P

NN = 8
NS = 4
BS = 64
PHYS = 4
ITERS = 4
NB = 32
FLAT = BS * BS
CHARGE_NUMBER = (0, 1, 1, 2)
CHARGE_SPIN = (0, 1, -1, 0)
OCCUPANCY = (0.0, 1.0, 1.0, 2.0)
STEP_SIZE = 0.06
EPSILON = 1e-06
HALF = PHYS // 2
LN = HALF * BS
F32, BF16 = jnp.float32, jnp.bfloat16
MIB = 2**20
VM = pl.BlockSpec(memory_space=pltpu.VMEM)
SM = pl.BlockSpec(memory_space=pltpu.SMEM)
HB = pl.BlockSpec(memory_space=pltpu.HBM)


def dot(a, b):
    return jnp.dot(a, b, preferred_element_type=F32)


def sector(q, number, spin):
    return (q // NS + number) % NN * NS + (q % NS + spin) % NS


def plus(q, s):
    return sector(q, CHARGE_NUMBER[s], CHARGE_SPIN[s])


def minus(q, s):
    return sector(q, -CHARGE_NUMBER[s], -CHARGE_SPIN[s])


def fold(x):
    total = x[0:8]
    for i in range(1, BS // 8):
        total = total + x[i * 8 : (i + 1) * 8]
    return total


def scaled_copy(src, factor):
    return (src.astype(F32) * factor).astype(BF16)


def krylov_kernel(second, core_of, *refs):
    if second:
        coup, kept, a_raw, b_even, b_odd, r_even, r_odd, left_raw = refs[:8]
        outs = refs[8:11]
        scratch = refs[11:]
    else:
        coup, kept, own, got, own_l, got_l, own_r, got_r = refs[:8]
        outs = refs[8:14]
        scratch = refs[14:]
    u, last, small = outs[:3]
    ab, lb, rb, bcat, w, sems, moments, b_raw, r_raw = scratch[:9]
    y = last
    core = core_of()

    if not second:
        at, a_flat, left_raw = outs[3:]
        a_raw = scratch[9]

    def moves(odd):
        if second:
            pairs = [
                (b_odd if odd else b_even, b_raw),
                (r_odd if odd else r_even, r_raw),
            ]
        else:
            t_a, t_b = (got, own) if odd else (own, got)
            pairs = [
                (t_a, a_raw),
                (t_b.at[pl.ds(HALF if odd else 0, HALF)], b_raw),
                (got_l if odd else own_l, left_raw),
                (own_r if odd else got_r, r_raw),
            ]
        return [pltpu.make_async_copy(x, z, sems.at[i]) for i, (x, z) in enumerate(pairs)]

    for odd in (False, True):

        @pl.when(core == int(odd))
        def _(odd=odd):
            for copy in moves(odd):
                copy.start()
            for copy in moves(odd):
                copy.wait()

    lane = lax.broadcasted_iota(jnp.int32, (1, LN), 1)
    rows16 = [
        jnp.where(lane < BS, coup[s1, core * HALF], coup[s1, core * HALF + 1]).astype(BF16)
        for s1 in range(PHYS)
    ]

    for ch in range(2):
        rb[...] = r_raw[ch].reshape(NB, BS, BS)
        for q in range(NB):
            for h in range(HALF):
                low, high = plus(q, h), plus(q, HALF + h)
                block = rb[low + core * (high - low)]
                zero = jnp.zeros((BS, BS), BF16)
                parts = [block, zero] if h == 0 else [zero, block]
                w[q, ch * LN + h * BS : ch * LN + (h + 1) * BS] = jnp.concatenate(parts, 1)
    for ch in range(2):
        lb[:, :, ch * BS : (ch + 1) * BS] = left_raw[ch].reshape(NB, BS, BS)
    for h in range(HALF):
        bcat[:, :, h * BS : (h + 1) * BS] = b_raw[h].reshape(NB, BS, BS)

    for s in range(PHYS):
        x = a_raw[s]
        if not second:
            a_flat[s] = x
        ab[s] = x.reshape(NB, BS, BS)

    for q in range(NB):
        if not second:
            for s1 in range(PHYS):
                at[q, :, s1 * BS : (s1 + 1) * BS] = ab[s1, minus(q, s1)].T
        lhs = jnp.concatenate([ab[s1, minus(q, s1)] for s1 in range(PHYS)], 0)
        out = dot(lhs, bcat[q]).astype(BF16)
        for s1 in range(PHYS):
            u[0, s1, minus(q, s1)] = out[s1 * BS : (s1 + 1) * BS]

    def product(it, _):
        now, later = u.at[it], u.at[it + 1]
        for q in range(NB):
            x = jnp.concatenate([now[s1, minus(q, s1)] for s1 in range(PHYS)], 0)
            c = jnp.concatenate([now[s1, minus(q, s1)] * rows16[s1] for s1 in range(PHYS)], 0)
            out = dot(jnp.concatenate([x, c], 1), w[q])
            for s1 in range(PHYS):
                y[s1, minus(q, s1)] = out[s1 * BS : (s1 + 1) * BS]
        even = jnp.zeros((8, LN), F32)
        odd = jnp.zeros((8, LN), F32)
        for q in range(NB):
            for pair in range(PHYS // 2):
                xs = [now[pair * 2 + j, q] for j in range(2)]
                cs = [xs[j] * rows16[pair * 2 + j] for j in range(2)]
                rhs = jnp.concatenate([jnp.concatenate(xs, 1), jnp.concatenate(cs, 1)], 0)
                out = dot(lb[q], rhs)
                for j in range(2):
                    s1 = pair * 2 + j
                    old = xs[j].astype(F32)
                    new = old - STEP_SIZE * (out[:, j * LN : (j + 1) * LN] + y[s1, q])
                    y[s1, q] = new
                    later[s1, q] = new.astype(BF16)
                    even = even + fold(old * old)
                    odd = odd + fold(old * new)
        moments[2 * it] = even
        moments[2 * it + 1] = odd
        return 0

    lax.fori_loop(0, ITERS, product, 0)

    row = lax.broadcasted_iota(jnp.int32, (8, 128), 0)
    column = lax.broadcasted_iota(jnp.int32, (8, 128), 1)
    out = jnp.zeros((8, 128), F32)
    for k in range(2 * ITERS):
        out = jnp.where((row == 0) & (column == k), jnp.sum(moments[k], keepdims=True), out)
    for q in range(NB):
        out = jnp.where((row == 1) & (column == q), kept[0, q].astype(F32), out)
    small[...] = out


def project_kernel(owner, core_of, own, got, u, last, at, x_out, v, xb):
    core = core_of()
    mine, other = own[...], got[...]
    both = mine + other
    row = lax.broadcasted_iota(jnp.int32, (8, 128), 0)
    column = lax.broadcasted_iota(jnp.int32, (8, 128), 1)

    def entry(array, r, c):
        return jnp.sum(jnp.where((row == r) & (column == c), array, 0.0), keepdims=True)

    t = [entry(both, 0, k) for k in range(2 * ITERS)]
    a = [jnp.ones((1, 1), F32)]
    for it in range(ITERS):
        den = sum(a[k] * a[j] * t[k + j] for k in range(it + 1) for j in range(it + 1))
        num = sum(a[k] * a[j] * t[k + j + 1] for k in range(it + 1) for j in range(it + 1))
        delta = 1.0 - num / den
        a = (
            [delta * a[0]]
            + [a[k - 1] + delta * a[k] for k in range(1, it + 1)]
            + [a[it]]
        )
    kept = jnp.where(core == owner, mine, other)
    row_ids = lax.broadcasted_iota(jnp.int32, (BS, LN), 0).astype(F32)
    for p in range(NB):
        parts = []
        for s1 in range(PHYS):
            q = minus(p, s1)
            total = last[s1, q]
            for k in range(ITERS):
                total = total + a[k] * u[k, s1, q].astype(F32)
            parts.append(total.astype(BF16))
        out = dot(at[p], jnp.concatenate(parts, 0))
        out = jnp.where(row_ids < entry(kept, 1, p), out, 0.0).astype(BF16)
        for h in range(HALF):
            xb[h, p] = out[:, h * BS : (h + 1) * BS]
    for h in range(HALF):
        x_out[h] = xb[h].reshape(NB, FLAT)


def env_part(left, at, env, ab, lb, hb, eb):
    mixed = (left[0].astype(F32) + left[1].astype(F32)).astype(BF16)
    lb[:, :, :BS] = mixed.reshape(NB, BS, BS)
    for q in range(NB):
        lhs = jnp.concatenate(
            [at[plus(q, s), :, s * BS : (s + 1) * BS] for s in range(PHYS)], 0
        )
        out = dot(lhs, lb[q]).astype(BF16)
        for s in range(PHYS):
            hb[s, q] = out[s * BS : (s + 1) * BS]
    for p in range(NB):
        halves = [hb[s, minus(p, s)] for s in range(PHYS)]
        energy = jnp.concatenate([half[:, :BS] for half in halves], 1)
        density = jnp.concatenate(
            [half[:, BS:] * BF16(OCCUPANCY[s]) for s, half in enumerate(halves)], 1
        )
        stack = jnp.concatenate([ab[s, minus(p, s)] for s in range(PHYS)], 0)
        out = dot(jnp.concatenate([energy, density], 0), stack) * (1.0 / (PHYS * BS))
        out = out.astype(BF16)
        eb[0, p] = out[:BS]
        eb[1, p] = out[BS:]
    for ch in range(2):
        env[ch] = eb[ch].reshape(NB, FLAT)


def env_kernel(a_flat, left, at, env, ab, lb, hb, eb):
    for s in range(PHYS):
        ab[s] = a_flat[s].reshape(NB, BS, BS)
    lb[:, :, BS:] = left[1].reshape(NB, BS, BS)
    env_part(left, at, env, ab, lb, hb, eb)


def sum_squares(ref, states):
    total = jnp.zeros((8, 128), F32)
    for s in range(states):
        for t in range(FLAT // 128):
            x = ref[s, :, t * 128 : (t + 1) * 128].astype(F32)
            x = x * x
            total = total + (x[0:8] + x[8:16]) + (x[16:24] + x[24:32])
    return total


def norm_factor(total):
    return lax.rsqrt(jnp.sum(total, keepdims=True) / (PHYS * NB * FLAT) + EPSILON)


def prepare_kernel(core_of, own, got, left, new, at, env, ab, lb, hb, eb):
    core = core_of()
    factor = norm_factor(sum_squares(own, HALF) + sum_squares(got, HALF))
    for h in range(HALF):
        new[core * HALF + h] = scaled_copy(own[h], factor)
        new[(1 - core) * HALF + h] = scaled_copy(got[h], factor)
    for s in range(PHYS):
        ab[s] = new[s].reshape(NB, BS, BS)
    for q in range(NB):
        for s1 in range(PHYS):
            at[q, :, s1 * BS : (s1 + 1) * BS] = ab[s1, minus(q, s1)].T
    lb[:, :, BS:] = left[1].reshape(NB, BS, BS)
    env_part(left, at, env, ab, lb, hb, eb)


def choose_kernel(tensor, new, low, high, left, env, got_env, out, out_env):
    odd = lax.rem(lax.axis_index("site"), 2) == 1
    first = jnp.logical_and(lax.axis_index("site") == 0, lax.axis_index("sec") == 0)

    @pl.when(odd)
    def _():
        out[...] = new[...]
        out_env[...] = env[...]

    @pl.when(first)
    def _():
        out[...] = tensor[...]
        out_env[...] = left[...]

    @pl.when(jnp.logical_not(jnp.logical_or(odd, first)))
    def _():
        factor = norm_factor(sum_squares(low, HALF) + sum_squares(high, HALF))
        for s in range(HALF):
            out[s] = scaled_copy(low[s], factor)
            out[HALF + s] = scaled_copy(high[s], factor)
        out_env[...] = got_env[...]


def shape(*dims, dtype=BF16):
    return jax.ShapeDtypeStruct(dims, dtype)


def params(size):
    return pltpu.CompilerParams(vmem_limit_bytes=size * MIB)


def krylov(core_of, second, coupling, kept, *arrays):
    outs = [
        shape(ITERS + 1, PHYS, NB, BS, LN),
        shape(PHYS, NB, BS, LN, dtype=F32),
        shape(8, 128, dtype=F32),
    ]
    if not second:
        outs += [shape(NB, BS, PHYS * BS), shape(PHYS, NB, FLAT), shape(2, NB, FLAT)]
    scratch = [
        pltpu.VMEM((PHYS, NB, BS, BS), BF16),
        pltpu.VMEM((NB, BS, 2 * BS), BF16),
        pltpu.VMEM((NB, BS, BS), BF16),
        pltpu.VMEM((NB, BS, LN), BF16),
        pltpu.VMEM((NB, 2 * LN, LN), BF16),
        pltpu.SemaphoreType.DMA((4,)),
        pltpu.VMEM((2 * ITERS, 8, LN), F32),
        pltpu.VMEM((HALF, NB, FLAT), BF16),
        pltpu.VMEM((2, NB, FLAT), BF16),
    ]
    if second:
        specs = [SM, SM, VM] + [HB] * 4 + [VM]
    else:
        specs = [SM, SM] + [HB] * 6
        scratch.append(pltpu.VMEM((PHYS, NB, FLAT), BF16))
    return pl.pallas_call(
        functools.partial(krylov_kernel, second, core_of),
        out_shape=tuple(outs),
        in_specs=specs,
        out_specs=(VM,) * len(outs),
        scratch_shapes=scratch,
        compiler_params=params(28),
        cost_estimate=pl.CostEstimate(flops=10**11, bytes_accessed=2**24, transcendentals=0),
        name="krylov",
    )(coupling, kept, *arrays)


def project(core_of, owner, own, got, u, last, at):
    return pl.pallas_call(
        functools.partial(project_kernel, owner, core_of),
        out_shape=shape(HALF, NB, FLAT),
        in_specs=[VM] * 5,
        out_specs=VM,
        scratch_shapes=[
            pltpu.VMEM((8, 128), F32),
            pltpu.VMEM((HALF, NB, BS, BS), BF16),
        ],
        compiler_params=params(20),
        cost_estimate=pl.CostEstimate(flops=10**6, bytes_accessed=2**10, transcendentals=0),
        name="project",
    )(own, got, u, last, at)


def grow(a_flat, left, at):
    return pl.pallas_call(
        env_kernel,
        out_shape=shape(2, NB, FLAT),
        in_specs=[VM] * 3,
        out_specs=VM,
        scratch_shapes=[
            pltpu.VMEM((PHYS, NB, BS, BS), BF16),
            pltpu.VMEM((NB, BS, 2 * BS), BF16),
            pltpu.VMEM((PHYS, NB, BS, 2 * BS), BF16),
            pltpu.VMEM((2, NB, BS, BS), BF16),
        ],
        compiler_params=params(12),
        cost_estimate=pl.CostEstimate(flops=10**6, bytes_accessed=2**10, transcendentals=0),
        name="grow",
    )(a_flat, left, at)


def prepare(core_of, own, got, left):
    return pl.pallas_call(
        functools.partial(prepare_kernel, core_of),
        out_shape=(
            shape(PHYS, NB, FLAT),
            shape(NB, BS, PHYS * BS),
            shape(2, NB, FLAT),
        ),
        in_specs=[VM] * 3,
        out_specs=(VM,) * 3,
        scratch_shapes=[
            pltpu.VMEM((PHYS, NB, BS, BS), BF16),
            pltpu.VMEM((NB, BS, 2 * BS), BF16),
            pltpu.VMEM((PHYS, NB, BS, 2 * BS), BF16),
            pltpu.VMEM((2, NB, BS, BS), BF16),
        ],
        compiler_params=params(12),
        cost_estimate=pl.CostEstimate(flops=10**6, bytes_accessed=2**10, transcendentals=0),
        name="prepare",
    )(own, got, left)


def choose(*arrays):
    return pl.pallas_call(
        choose_kernel,
        out_shape=(shape(PHYS, NB, FLAT), shape(2, NB, FLAT)),
        in_specs=[VM] * 7,
        out_specs=(VM, VM),
        compiler_params=params(12),
        name="choose",
    )(*arrays)


def core_index():
    return lax.rem(lax.axis_index("site"), 2)


def shards(tensors, left_env, right_env, kept_rows, coupling):
    across = lax.axis_size("site")
    count = lax.axis_size("sec") * across
    axes = ("sec", "site")
    tensor, left, right = tensors[0], left_env[0], right_env[0]

    swap = [(i, i ^ 1) for i in range(count)]
    rise = [(i, i + 1) for i in range(0, count, 2)]
    fall = [(i + 1, i) for i in range(0, count, 2)]
    to_even = [(i, i - 2) for i in range(2, count, 2)]
    to_odd = [(i, i - 1) for i in range(2, count, 2)]
    from_even = [(i, i + 2) for i in range(0, count - 2, 2)]
    from_odd = [(i, i + 1) for i in range(1, count - 2, 2)]

    def send(x, pairs):
        return lax.ppermute(x, axes, pairs)

    got_t = send(tensor, swap)
    got_l = send(left, rise)
    got_r = send(right, fall)
    low, high, late_r, got_t, got_l, got_r = lax.optimization_barrier(
        (tensor[:HALF], tensor[HALF:], right, got_t, got_l, got_r)
    )
    b_even = send(low, to_even)
    b_odd = send(high, to_odd)
    r_odd = send(late_r, to_odd)

    u, last, small, at, a_flat, l_flat = krylov(
        core_index, False, coupling, kept_rows, tensor, got_t, left, got_l, right, got_r
    )
    got_small = send(small, swap)
    env1 = grow(a_flat, l_flat, at)
    x = project(core_index, 0, small, got_small, u, last, at)
    x, b_even, b_odd, r_odd = lax.optimization_barrier((x, b_even, b_odd, r_odd))
    got_x = send(x, swap)
    r_even = send(r_odd, fall)

    new1, at, env2 = prepare(core_index, x, got_x, env1)
    got_env = send(env2, from_odd)
    u, last, small = krylov(
        core_index, True, coupling, kept_rows, new1, b_even, b_odd, r_even, r_odd, env1
    )
    got_small = send(small, swap)
    x = project(core_index, 1, small, got_small, u, last, at)
    x, got_env = lax.optimization_barrier((x, got_env))
    low = send(x, from_even)
    high = send(x, from_odd)
    got_env, low, high = lax.optimization_barrier((got_env, low, high))

    out_new, out_env = choose(tensor, new1, low, high, left, env1, got_env)
    return out_new[None], out_env[None]


def solution(mesh):
    sites = P(("sec", "site"), None, None, None)
    return jax.shard_map(
        shards,
        mesh=mesh,
        in_specs=(sites, sites, sites, P(("sec", "site"), None), P()),
        out_specs=(sites, sites),
        check_vma=False,
    )
```
